256 devices in a mesh: dp: 4 (over x), shard: 64 (over y, z, core).
Axes of the slice: x: 4, y: 4, z: 8, core: 2. Of those that a mesh axis runs over, the one named last changes fastest.
Arguments:
- partial_grads: float32 [4, 112, 768, 1024], P('dp', None, 'shard'), may hold values from -60 to 60
- momentum: float32 [112, 768, 1024], P('dp', 'shard'), may hold values from -6 to 6
- owners: int32 [112], replicated, may hold values from 0 to 63, as said below
Outputs:
- new_momentum: float32 [112, 768, 1024], P('dp', 'shard')
- update: float32 [112, 768, 1024], P('dp', 'shard')
- owned: bfloat16 [4, 64, 768, 1024], P('dp', 'shard')
The draws below stay inside these ranges and needn't reach their ends.
Inputs may be any that keep to these rules, and one draw needn't show every extreme that they name: Entries 28 * p to 28 * (p + 1) - 1 name the owners of the matrices that the p-th index of dp holds after the sum. No owner gets more than 1 matrices of one group, and in every group some owner gets exactly 1.
All inputs are finite; a program needn't handle non-finite values.
Results may differ from the reference program's by a relative error of at most 0.014.
Values may be sent and summed in bfloat16 or wider, within the bound.
A program may use at most 64 MiB of HBM per device.

```python
import math
import jax
import jax.numpy as jnp
from jax import lax

D = 1024
F = 768
M_ROW = 28
ITERS = 2
CAP = 1
M = 112
N_DP = 4
N_SHARD = 64


def draw_partial_grads(key, part):
    key = jax.random.fold_in(key, 11)
    key_rows = jax.random.fold_in(key, 0)
    key_cols = jax.random.fold_in(key, 1)
    key_own = jax.random.fold_in(key, 3)
    row_scale = jnp.exp(jax.random.uniform(key_rows, (1, M, F, 1), jnp.float32) * math.log(10.0))
    col_scale = jnp.exp(jax.random.uniform(key_cols, (1, M, 1, D), jnp.float32) * math.log(10.0))
    noise = 0.1 * jnp.clip(jax.random.normal(key_own, (N_DP, M, F, D), jnp.float32), -6.0, 6.0)
    return (noise * row_scale * col_scale).astype(jnp.float32)


def draw_owners(key, part):
    key = jax.random.fold_in(key, 5)
    pieces = []
    most_full = M_ROW // CAP
    for group_index in range(N_DP):
        key_owner, key_order, key_full = jax.random.split(jax.random.fold_in(key, group_index), 3)
        owner_perm = jax.random.permutation(key_owner, N_SHARD)
        order_perm = jax.random.permutation(key_order, M_ROW)
        full_count = jax.random.randint(key_full, (), 1, most_full + 1).astype(jnp.int32)
        position = jnp.arange(M_ROW, dtype=jnp.int32)
        rest_owners = jnp.maximum(N_SHARD - full_count, 1).astype(jnp.int32)
        rest_slot = full_count + (position - full_count * CAP) % rest_owners
        source_slot = jnp.where(position < full_count * CAP, position // CAP, rest_slot)
        source_slot = jnp.clip(source_slot, 0, N_SHARD - 1).astype(jnp.int32)
        owner_by_position = owner_perm[source_slot]
        owner_row = jnp.zeros((M_ROW,), jnp.int32).at[order_perm].set(owner_by_position.astype(jnp.int32))
        pieces.append(owner_row)
    return jnp.concatenate(pieces).astype(jnp.int32)


def shard_levels(rng, extent, cuts, least, high):
    gain, own = 1.0, jax.random.fold_in(rng, 6)
    for axis_at, shards_of in cuts:
        draws = jnp.exp(jax.random.uniform(jax.random.fold_in(own, axis_at), (shards_of,), jnp.float32, least / len(cuts), high / len(cuts)))
        gain = gain * jnp.repeat(draws, extent[axis_at] // shards_of).reshape([-1 if axis == axis_at else 1 for axis in range(len(extent))])
    return gain


def normal_values(rng, dims, spread, most, cuts=(), kind=jnp.bfloat16):
    drawn = spread * jax.random.normal(rng, dims, jnp.float32)
    if cuts:
        drawn = drawn * shard_levels(rng, dims, cuts, -0.22, 0.18)
    return jnp.clip(drawn, -most, most).astype(kind)


def setup_inputs(seed: int = 0) -> dict:
    key_list = jax.random.split(jax.random.key(seed), 4)
    partial_grads = draw_partial_grads(jax.random.fold_in(key_list[3], 71), 0)
    momentum = normal_values(key_list[1], (M, F, D), 1.0, 6.0, ((0, 4), (1, 64)), jnp.float32)
    owners = draw_owners(jax.random.fold_in(key_list[3], 71), 0)
    return {"partial_grads": partial_grads, "momentum": momentum, "owners": owners}


momentum_decay = 0.95
epsilon_norm = 1e-07
coeff_first = 3.4445
coeff_second = -4.775
coeff_third = 2.0315

def orthogonalize_one(matrix):
    widened = matrix.astype(jnp.float32)
    frobenius = jnp.sqrt(jnp.sum(widened * widened))
    iterate = (widened / (frobenius + epsilon_norm)).astype(jnp.bfloat16)
    for sweep in range(ITERS):
        gram_matrix = jnp.dot(iterate, iterate.T, preferred_element_type=jnp.float32).astype(jnp.bfloat16)
        gram_square = jnp.dot(gram_matrix, gram_matrix, preferred_element_type=jnp.float32)
        poly_term = (coeff_second * gram_matrix.astype(jnp.float32) + coeff_third * gram_square).astype(jnp.bfloat16)
        product = jnp.dot(poly_term, iterate, preferred_element_type=jnp.float32)
        iterate = (coeff_first * iterate.astype(jnp.float32) + product).astype(jnp.bfloat16)
    return iterate

def reference(partial_grads, momentum, owners):
    gradient = lax.optimization_barrier(jnp.sum(partial_grads, axis=0))
    new_momentum = momentum_decay * momentum + gradient
    nesterov = (gradient + momentum_decay * new_momentum).astype(jnp.bfloat16)
    orthogonal = lax.map(orthogonalize_one, nesterov)
    update = orthogonal.astype(jnp.float32) * (0.2 * math.sqrt(max(F, D)))
    owner_rows = owners.reshape(N_DP, M_ROW).astype(jnp.int32)
    local_index = jnp.arange(M_ROW, dtype=jnp.int32)
    earlier_same = (owner_rows[:, :, None] == owner_rows[:, None, :]) & (local_index[None, None, :] < local_index[None, :, None])
    slot_rows = lax.optimization_barrier(jnp.sum(earlier_same.astype(jnp.int32), axis=2)).astype(jnp.int32)
    target_rows = (owner_rows * CAP + slot_rows).reshape(M).astype(jnp.int32)
    group_rows = (jnp.arange(M, dtype=jnp.int32) // M_ROW).astype(jnp.int32)
    owned = jnp.zeros((N_DP, N_SHARD * CAP, F, D), orthogonal.dtype).at[group_rows, target_rows].set(orthogonal)
    return (new_momentum, update, owned)
```

```python
import functools
import math

import jax
import jax.numpy as jnp
from jax import lax
from jax.experimental import pallas as pl
from jax.experimental.pallas import tpu as pltpu
from jax.sharding import PartitionSpec as P


MESH = pl.DeviceIdType.MESH
BF = jnp.bfloat16
F32 = jnp.float32
I32 = jnp.int32

D, F = 1024, 768
NX, NY, NZ = 4, 4, 8
MROW = 28
CHUNKS, WIDE = 4, 256
HALF = WIDE // 2
SLOTS = 4
SCALE = 0.2 * math.sqrt(max(F, D))

momentum_decay = 0.95
epsilon_norm = 1e-07
coeff_first = 3.4445
coeff_second = -4.775
coeff_third = 2.0315


def iota(shape, axis):
    return lax.broadcasted_iota(I32, shape, axis)


def onehot(cond):
    return jnp.where(cond, 1.0, 0.0).astype(BF)


def dot(a, b):
    return jnp.dot(a, b, preferred_element_type=F32)


def dot_t(a, b):
    return lax.dot_general(a, b, (((1,), (1,)), ((), ())), preferred_element_type=F32)


def routes(owner, z_here):
    r0, r1 = iota((128, 128), 0), iota((128, 128), 1)
    owner = jnp.broadcast_to(owner[0:1], (128, 128))
    valid = r1 < MROW
    plane = jnp.where(valid, (owner >> 1) & 7, 99).astype(F32)
    place = jnp.where(valid, ((owner >> 4) << 1) | (owner & 1), 99).astype(F32)
    diag, before = r0 == r1, r0 < r1

    def column(row):
        return jnp.sum(jnp.where(diag, row, 0.0), axis=1, keepdims=True)

    def total(cond):
        return jnp.sum(jnp.where(cond, 1.0, 0.0), axis=0, keepdims=True)

    rank = total((column(plane) == plane) & before)
    valid = valid[0:1]
    home = valid & (rank < SLOTS)
    over = valid & (rank >= SLOTS)
    over_f = jnp.where(over, 1.0, 0.0)
    nth = total((column(jnp.broadcast_to(over_f, (128, 128))) > 0.5) & before)
    r0f = r0.astype(F32)
    count = jnp.sum(jnp.where(plane == r0f, 1.0, 0.0), axis=1, keepdims=True)
    taken = jnp.minimum(count, float(SLOTS))
    free = jnp.where(r0[:, 0:1] < NZ, float(SLOTS) - taken, 0.0)
    free_row = jnp.sum(jnp.where(diag, free, 0.0), axis=0, keepdims=True)
    first = jnp.sum(jnp.where(r1 < r0, free_row, 0.0), axis=1, keepdims=True)
    hit = (first <= nth) & (nth < first + free) & (r0 < NZ)
    away = jnp.sum(jnp.where(hit, r0f * SLOTS + taken + nth - first, 0.0), axis=0, keepdims=True)
    plane_row = plane[0:1]
    code = jnp.where(home, plane_row * SLOTS + rank, jnp.where(over, away, -1.0))
    code_over = jnp.where(over, plane_row * SLOTS + rank - SLOTS, -1.0)

    def tiled(row):
        row = jnp.where(valid, row, -1.0)
        wide = jnp.broadcast_to(row, (8, 128))
        out = wide
        for turn in (1, 2, 3):
            lane = iota((8, 128), 1)
            out = jnp.where((lane >> 5) == turn, pltpu.roll(wide, 32 * turn, 1), out)
        return out[0:1]

    same_row = ((r0 >> 2) & 3) == (r1 >> 5)
    wanted = ((r0 >> 4) * SLOTS + (r0 & 3)).astype(F32)
    forward = onehot(same_row & (tiled(code) == wanted))
    forward_over = onehot(same_row & (tiled(code_over) == wanted))
    code_col = jnp.sum(
        jnp.where(r1 == (r0 & 31), jnp.broadcast_to(code, (128, 128)), 0.0), axis=1, keepdims=True
    )
    code_col = jnp.where((r0[:, 0:1] & 31) < MROW, code_col, -1.0)
    back = onehot(
        ((r0 >> 5) == ((r1 >> 2) & 3)) & (code_col == ((r1 >> 4) * SLOTS + (r1 & 3)).astype(F32))
    )
    e0, e1 = iota((256, 128), 0), iota((256, 128), 1)
    mine = (place[0:1] == (e0 >> 5).astype(F32)) & (plane_row == z_here.astype(F32))
    pick = jnp.sum(jnp.where(mine, rank + 1.0, 0.0), axis=1, keepdims=True) - 1.0
    match = (((e0 >> 2) & 7) == (e1 >> 4)) & ((e0 & 3) == ((e1 >> 2) & 3))
    slot = (e1 & 3).astype(F32)
    give = onehot(match & (pick == slot))
    give_over = onehot(match & (pick == slot + SLOTS))
    return forward, forward_over, back, give, give_over


def kernel(
    grads_hbm,
    momentum_hbm,
    owners_ref,
    newm_ref,
    update_ref,
    owned_ref,
    grads,
    momentum,
    s_direct,
    s_far,
    s_comb,
    r_direct,
    r_far,
    r_comb,
    part,
    own,
    nest,
    zs_f,
    zr_f,
    zs_o,
    zr_o,
    zs_r,
    zr_r,
    ys_p,
    x_p,
    ys_r,
    yr_r,
    ys_o,
    x_o,
    x_a,
    x_b,
    gram_f,
    gram_b,
    poly_b,
    m_forward,
    m_over,
    m_back,
    m_give,
    m_give_over,
    load_sem,
    x_send,
    direct_sem,
    far_sem,
    comb_sem,
    z_send,
    zf_sem,
    zo_sem,
    zr_sem,
    y_send,
    yp_sem,
    yr_sem,
    yo_sem,
):
    x = lax.axis_index("dp")
    here = lax.axis_index("shard")
    y, z, c = here // 16, (here // 2) % NZ, here % 2
    e = 2 * y + c
    right, left, far = (x + 1) % NX, (x + 3) % NX, (x + 2) % NX

    def at(y_, z_, c_):
        return (x, (y_ * NZ + z_) * 2 + c_)

    def send(src, dst, send_sem, recv_sem, device):
        pltpu.make_async_remote_copy(
            src_ref=src, dst_ref=dst, send_sem=send_sem, recv_sem=recv_sem,
            device_id=device, device_id_type=MESH,
        ).start()

    def wait_recv(ref, sem):
        pltpu.make_async_remote_copy(
            src_ref=ref, dst_ref=ref, send_sem=sem, recv_sem=sem,
            device_id=(x, here), device_id_type=MESH,
        ).wait_recv()

    def wait_send(ref, sem):
        pltpu.make_async_remote_copy(
            src_ref=ref, dst_ref=ref, send_sem=sem, recv_sem=sem,
            device_id=(x, here), device_id_type=MESH,
        ).wait_send()

    def load(k):
        return pltpu.make_async_copy(
            grads_hbm.at[:, :, pl.ds(k * WIDE, WIDE)], grads.at[k], load_sem.at[k]
        )

    load_momentum = pltpu.make_async_copy(momentum_hbm, momentum, load_sem.at[CHUNKS])
    for k in range(CHUNKS):
        load(k).start()
    load_momentum.start()

    barrier = pltpu.get_barrier_semaphore()
    for device in ((right, here), (left, here)):
        pl.semaphore_signal(barrier, 1, device_id=device, device_id_type=MESH)
    for step in range(1, NZ):
        pl.semaphore_signal(barrier, 1, device_id=at(y, (z + step) % NZ, c), device_id_type=MESH)
    for step in range(1, 8):
        other = (e + step) % 8
        pl.semaphore_signal(
            barrier, 1, device_id=at(other // 2, z, other % 2), device_id_type=MESH
        )

    owner = pltpu.roll(jnp.broadcast_to(owners_ref[...], (8, 128)), (128 - MROW * x) % 128, 1)
    forward, forward_over, back, give, give_over = routes(owner, z)
    m_forward[...] = forward
    m_over[...] = forward_over
    m_back[...] = back
    m_give[...] = give
    m_give_over[...] = give_over
    nest[...] = jnp.zeros_like(nest)

    p0, p1 = iota((112, 128), 0), iota((112, 128), 1)
    quarter = (
        jnp.where(p0 >= 28, 1, 0) + jnp.where(p0 >= 56, 1, 0) + jnp.where(p0 >= 84, 1, 0)
    )

    def packing(parity):
        return onehot(p1 == p0 + 4 * quarter + 4 * parity)

    def window(k, to, table, g):
        start = pl.multiple_of(((MROW * to) // 8) * 8, 8)
        rows = grads[k, 4 * g : 4 * g + 4, pl.ds(start, 32), :].astype(BF).reshape(128, WIDE)
        return dot(table, rows)

    def pack(k):
        load(k).wait()
        odd = packing((x + 1) % 2)
        even = packing(x % 2)
        for g in range(3):
            v = window(k, far, even, g).astype(BF)
            s_far[0, k, g] = v[:, :HALF]
            s_far[1, k, g] = v[:, HALF:]
            v = window(k, right, odd, g)
            part[0, k, g] = v[:, :HALF]
            s_direct[0, k, g] = v[:, HALF:].astype(BF)
            v = window(k, left, odd, g)
            part[1, k, g] = v[:, HALF:]
            s_direct[1, k, g] = v[:, :HALF].astype(BF)

    def pack_own(k):
        even = packing(x % 2)
        for g in range(3):
            own[k, g] = window(k, x, even, g)

    towards = ((right, here), (left, here))

    def send_first(k):
        for way in range(2):
            send(s_far.at[way, k], r_far.at[way, k], x_send.at[0], far_sem.at[way, k], towards[way])
        for way in range(2):
            send(
                s_direct.at[way, k], r_direct.at[way, k], x_send.at[1], direct_sem.at[way, k],
                towards[way],
            )

    def send_combined(k):
        for way in range(2):
            wait_recv(r_far.at[way, k], far_sem.at[way, k])
            s_comb[way, k] = (part[way, k] + r_far[way, k].astype(F32)).astype(BF)
            send(
                s_comb.at[way, k], r_comb.at[way, k], x_send.at[2], comb_sem.at[way, k],
                towards[way],
            )

    def gradient(k):
        for way in range(2):
            wait_recv(r_direct.at[way, k], direct_sem.at[way, k])
            wait_recv(r_comb.at[way, k], comb_sem.at[way, k])
        low = own[k, :, :, :HALF] + r_direct[1, k].astype(F32) + r_comb[0, k].astype(F32)
        high = own[k, :, :, HALF:] + r_direct[0, k].astype(F32) + r_comb[1, k].astype(F32)
        own[k, :, :, :HALF] = low
        own[k, :, :, HALF:] = high
        for g in range(3):
            for rr in range(4):
                total = own[k, g, MROW * rr : MROW * (rr + 1), :]
                cols = slice(k * WIDE, (k + 1) * WIDE)
                moved = momentum_decay * momentum[4 * g + rr, :, cols] + total
                newm_ref[4 * g + rr, :, cols] = moved
                nest[g, 32 * rr : 32 * rr + MROW, :] = total + momentum_decay * moved

    def send_z(zs, zr, k, sem, recv_sem):
        zr[k, pl.ds(z, 1)] = zs[k, pl.ds(z, 1)]
        for step in (1, 7, 2, 6, 3, 5, 4):
            to = (z + step) % NZ
            send(zs.at[k, to], zr.at[k, z], sem, recv_sem.at[k], at(y, to, c))

    def forward_z(k):
        for g in range(3):
            rows = nest[g].astype(BF)
            zs_f[k, :, g] = dot(m_forward[...], rows).astype(BF).reshape(NZ, 16, WIDE)
        send_z(zs_f, zr_f, k, z_send.at[0], zf_sem)
        for g in range(3):
            rows = nest[g].astype(BF)
            zs_o[k, :, g] = dot(m_over[...], rows).astype(BF).reshape(NZ, 16, WIDE)
        send_z(zs_o, zr_o, k, z_send.at[1], zo_sem)

    i0, i1 = iota((128, 128), 0), iota((128, 128), 1)
    to_slots = lambda: onehot(i1 == ((i0 & 31) << 2) + (i0 >> 5))
    from_slots = lambda: onehot(i0 == ((i1 & 31) << 2) + (i1 >> 5))

    def others(n, me):
        return [(me + step) % n for step in range(1, n)]

    def relay_p(k):
        wait_recv(zr_f.at[k, pl.ds(0, 7)], zf_sem.at[k])
        table = to_slots()
        for g in range(3):
            rows = zr_f[k, :, g].reshape(128, WIDE)
            ys_p[k, :, g] = dot(table, rows).astype(BF).reshape(SLOTS, 32, WIDE)
        for to in others(NY, y):
            send(ys_p.at[k, to], x_p.at[k, e], y_send.at[0], yp_sem.at[k], at(to, z, 0))

        @pl.when(c == 0)
        def _():
            x_p[k, pl.ds(e, 1)] = ys_p[k, pl.ds(y, 1)]

        @pl.when(c == 1)
        def _():
            send(ys_p.at[k, y], x_p.at[k, e], y_send.at[1], yp_sem.at[k], at(y, z, 0))

    def matrix(ref, k):
        return ref[k].reshape(F, WIDE)

    def add_gram(src, k):
        rows = matrix(src, k)
        new = dot_t(rows, rows)
        gram_f[...] = new if k == 0 else gram_f[...] + new
        wide = rows.astype(F32)
        return jnp.sum(wide * wide)

    def poly():
        for i in range(3):
            block = gram_b[256 * i : 256 * (i + 1), :]
            square = dot(block, gram_b[...])
            poly_b[256 * i : 256 * (i + 1), :] = (
                coeff_second * block.astype(F32) + coeff_third * square
            ).astype(BF)

    def advance(src, dst, k):
        rows = matrix(src, k)
        out = coeff_first * rows.astype(F32) + dot(poly_b[...], rows)
        dst[k] = out.astype(BF).reshape(8, 3, 32, WIDE)

    def finish(src, dst, squares, done):
        inverse = 1.0 / (jnp.sqrt(squares) + epsilon_norm)
        gram_b[...] = (gram_f[...] * (inverse * inverse)).astype(BF)
        for k in range(CHUNKS):
            x_a[k] = (src[k].astype(F32) * inverse).astype(BF)
        poly()
        for k in range(CHUNKS):
            advance(x_a, x_b, k)
        for k in range(CHUNKS):
            add_gram_only(k)
        gram_b[...] = gram_f[...].astype(BF)
        poly()
        for k in range(CHUNKS):
            advance(x_b, dst, k)
            done(k)

    def add_gram_only(k):
        rows = matrix(x_b, k)
        new = dot_t(rows, rows)
        gram_f[...] = new if k == 0 else gram_f[...] + new

    def send_back(k):
        yr_r[k, pl.ds(y, 1)] = ys_r[k, pl.ds(e, 1)]
        for to in others(8, e):
            send(ys_r.at[k, to], yr_r.at[k, y], y_send.at[2], yr_sem.at[k], at(to // 2, z, to % 2))

    def primary():
        squares = 0.0
        for k in range(CHUNKS):
            wait_recv(x_p.at[k, pl.ds(0, 7)], yp_sem.at[k])
            squares = squares + add_gram(x_p, k)
        finish(x_p, ys_r, squares, send_back)

    def relay_o(k):
        wait_recv(zr_o.at[k, pl.ds(0, 7)], zo_sem.at[k])
        for g in range(3):
            rows = dot(m_give[...], zr_f[k, :, g].reshape(128, WIDE)) + dot(
                m_give_over[...], zr_o[k, :, g].reshape(128, WIDE)
            )
            ys_o[k, :, g] = rows.astype(BF).reshape(8, 32, WIDE)
        x_o[k, pl.ds(e, 1)] = ys_o[k, pl.ds(e, 1)]
        for to in others(8, e):
            send(ys_o.at[k, to], x_o.at[k, e], y_send.at[3], yo_sem.at[k], at(to // 2, z, to % 2))

    def relay_r(k):
        @pl.when(c == 0)
        def _():
            wait_recv(yr_r.at[k, pl.ds(0, 3)], yr_sem.at[k])

        @pl.when(c == 1)
        def _():
            wait_recv(yr_r.at[k, pl.ds(0, 4)], yr_sem.at[k])

        table = from_slots()
        for g in range(3):
            rows = yr_r[k, :, g].reshape(128, WIDE)
            zs_r[k, :, g] = dot(table, rows).astype(BF).reshape(NZ, 16, WIDE)
        send_z(zs_r, zr_r, k, z_send.at[2], zr_sem)

    def owner_part():
        squares = 0.0
        for k in range(CHUNKS):
            wait_recv(x_o.at[k, pl.ds(0, 7)], yo_sem.at[k])
            squares = squares + add_gram(x_o, k)

        t0, t1 = iota((192, 192), 0), iota((192, 192), 1)
        g0 = jnp.where((t1 % 96) >= 64, 2, jnp.where((t1 % 96) >= 32, 1, 0))
        c0 = jnp.where(t1 >= 96, 1, 0)
        place = ((t1 >> 2) & 7) * 24 + c0 * 12 + g0 * 4 + (t1 & 3)
        table = onehot(t0 == place)

        def done(k):
            for b in range(4):
                rows = x_a[k, 2 * b : 2 * b + 2].reshape(192, WIDE)
                owned_ref[192 * b : 192 * (b + 1), k * WIDE : (k + 1) * WIDE] = dot(
                    table, rows
                ).astype(BF)

        finish(x_o, x_a, squares, done)

    def unpack(k):
        wait_recv(zr_r.at[k, pl.ds(0, 7)], zr_sem.at[k])
        for g in range(3):
            rows = dot(m_back[...], zr_r[k, :, g].reshape(128, WIDE)) * SCALE
            rows = rows.reshape(4, 32, WIDE)
            update_ref[4 * g : 4 * g + 4, :, k * WIDE : (k + 1) * WIDE] = rows[:, :MROW, :]

    pack(0)
    pl.semaphore_wait(barrier, 16)
    send_first(0)
    pack(1)
    send_first(1)
    pack_own(0)
    load_momentum.wait()
    for k in range(CHUNKS):
        send_combined(k)
        if k + 2 < CHUNKS:
            pack(k + 2)
            send_first(k + 2)
        if k + 1 < CHUNKS:
            pack_own(k + 1)
        gradient(k)
        forward_z(k)
        if k >= 1:
            relay_p(k - 1)
    relay_p(CHUNKS - 1)

    @pl.when(c == 0)
    def _():
        primary()

    for k in range(CHUNKS):
        relay_o(k)
    for k in range(CHUNKS):
        relay_r(k)
    owner_part()
    for k in range(CHUNKS):
        unpack(k)

    wait_send(s_far, x_send.at[0])
    wait_send(s_direct, x_send.at[1])
    wait_send(s_comb, x_send.at[2])
    for i, ref in enumerate((zs_f, zs_o, zs_r)):
        wait_send(ref.at[:, pl.ds(0, 7)], z_send.at[i])
    wait_send(ys_p.at[:, pl.ds(0, 3)], y_send.at[0])

    @pl.when(c == 1)
    def _():
        wait_send(ys_p.at[:, 0], y_send.at[1])

    @pl.when(c == 0)
    def _():
        wait_send(ys_r.at[:, pl.ds(0, 7)], y_send.at[2])

    wait_send(ys_o.at[:, pl.ds(0, 7)], y_send.at[3])


def scratch():
    def vmem(*shape, dtype=BF):
        return pltpu.VMEM(shape, dtype)

    dma = pltpu.SemaphoreType.DMA
    x_half = (2, CHUNKS, 3, 112, HALF)
    z_all = (CHUNKS, NZ, 3, 16, WIDE)
    plane = (CHUNKS, 8, 3, 32, WIDE)
    quarter = (CHUNKS, SLOTS, 3, 32, WIDE)
    return [
        vmem(CHUNKS, 12, 112, WIDE, dtype=F32),
        vmem(12, MROW, D, dtype=F32),
        *[vmem(*x_half) for _ in range(6)],
        vmem(*x_half, dtype=F32),
        vmem(CHUNKS, 3, 112, WIDE, dtype=F32),
        vmem(3, 128, WIDE, dtype=F32),
        *[vmem(*z_all) for _ in range(6)],
        vmem(*quarter),
        vmem(*plane),
        vmem(*plane),
        vmem(*quarter),
        vmem(*plane),
        vmem(*plane),
        vmem(*plane),
        vmem(*plane),
        vmem(F, F, dtype=F32),
        vmem(F, F),
        vmem(F, F),
        vmem(128, 128),
        vmem(128, 128),
        vmem(128, 128),
        vmem(256, 128),
        vmem(256, 128),
        dma((CHUNKS + 1,)),
        dma((3,)),
        dma((2, CHUNKS)),
        dma((2, CHUNKS)),
        dma((2, CHUNKS)),
        dma((3,)),
        dma((CHUNKS,)),
        dma((CHUNKS,)),
        dma((CHUNKS,)),
        dma((4,)),
        dma((CHUNKS,)),
        dma((CHUNKS,)),
        dma((CHUNKS,)),
    ]


def local(partial_grads, momentum, owners):
    grads = jnp.transpose(partial_grads[0], (1, 0, 2))
    held = jnp.transpose(momentum, (1, 0, 2))
    owners = jnp.pad(owners, (0, 16)).reshape(1, 128)
    vmem = pl.BlockSpec(memory_space=pltpu.VMEM)
    anywhere = pl.BlockSpec(memory_space=pl.ANY)
    new_momentum, update, owned = pl.pallas_call(
        kernel,
        out_shape=(
            jax.ShapeDtypeStruct((12, MROW, D), F32),
            jax.ShapeDtypeStruct((12, MROW, D), F32),
            jax.ShapeDtypeStruct((F, D), BF),
        ),
        in_specs=[anywhere, anywhere, vmem],
        out_specs=(vmem, vmem, vmem),
        scratch_shapes=scratch(),
        compiler_params=pltpu.CompilerParams(
            collective_id=0, has_side_effects=True, vmem_limit_bytes=60 << 20
        ),
    )(grads, held, owners)
    return (
        jnp.transpose(new_momentum, (1, 0, 2)),
        jnp.transpose(update, (1, 0, 2)),
        owned[None, None],
    )


def solution(mesh):
    return jax.shard_map(
        local,
        mesh=mesh,
        in_specs=(P("dp", None, "shard", None), P("dp", "shard", None), P()),
        out_specs=(P("dp", "shard", None), P("dp", "shard", None), P("dp", "shard", None, None)),
        check_vma=False,
    )
```

```python
import functools
import math

import jax
import jax.numpy as jnp
from jax import lax
from jax.experimental import pallas as pl
from jax.experimental.pallas import tpu as pltpu
from jax.sharding import PartitionSpec as P


MESH = pl.DeviceIdType.MESH
BF = jnp.bfloat16
F32 = jnp.float32
I32 = jnp.int32

D, F = 1024, 768
NX, NY, NZ = 4, 4, 8
MROW = 28
CHUNKS, WIDE = 4, 256
HALF = NARROW = WIDE // 2
SLOTS = 4
PIECES = 4
SCALE = 0.2 * math.sqrt(max(F, D))

momentum_decay = 0.95
epsilon_norm = 1e-07
coeff_first = 3.4445
coeff_second = -4.775
coeff_third = 2.0315


def iota(shape, axis):
    return lax.broadcasted_iota(I32, shape, axis)


def onehot(cond):
    return jnp.where(cond, 1.0, 0.0).astype(BF)


def dot(a, b):
    return jnp.dot(a, b, preferred_element_type=F32)


def dot_t(a, b):
    return lax.dot_general(a, b, (((1,), (1,)), ((), ())), preferred_element_type=F32)


def routes(owner, z_here):
    r0, r1 = iota((128, 128), 0), iota((128, 128), 1)
    owner = jnp.broadcast_to(owner[0:1], (128, 128))
    valid = r1 < MROW
    plane = jnp.where(valid, (owner >> 1) & 7, 99).astype(F32)
    place = jnp.where(valid, ((owner >> 4) << 1) | (owner & 1), 99).astype(F32)
    diag, before = r0 == r1, r0 < r1

    def column(row):
        return jnp.sum(jnp.where(diag, row, 0.0), axis=1, keepdims=True)

    def total(cond):
        return jnp.sum(jnp.where(cond, 1.0, 0.0), axis=0, keepdims=True)

    rank = total((column(plane) == plane) & before)
    valid = valid[0:1]
    home = valid & (rank < SLOTS)
    over = valid & (rank >= SLOTS)
    over_f = jnp.where(over, 1.0, 0.0)
    nth = total((column(jnp.broadcast_to(over_f, (128, 128))) > 0.5) & before)
    r0f = r0.astype(F32)
    count = jnp.sum(jnp.where(plane == r0f, 1.0, 0.0), axis=1, keepdims=True)
    taken = jnp.minimum(count, float(SLOTS))
    free = jnp.where(r0[:, 0:1] < NZ, float(SLOTS) - taken, 0.0)
    free_row = jnp.sum(jnp.where(diag, free, 0.0), axis=0, keepdims=True)
    first = jnp.sum(jnp.where(r1 < r0, free_row, 0.0), axis=1, keepdims=True)
    hit = (first <= nth) & (nth < first + free) & (r0 < NZ)
    away = jnp.sum(jnp.where(hit, r0f * SLOTS + taken + nth - first, 0.0), axis=0, keepdims=True)
    plane_row = plane[0:1]
    code = jnp.where(home, plane_row * SLOTS + rank, jnp.where(over, away, -1.0))
    code_over = jnp.where(over, plane_row * SLOTS + rank - SLOTS, -1.0)

    def tiled(row):
        row = jnp.where(valid, row, -1.0)
        wide = jnp.broadcast_to(row, (8, 128))
        out = wide
        for turn in (1, 2, 3):
            lane = iota((8, 128), 1)
            out = jnp.where((lane >> 5) == turn, pltpu.roll(wide, 32 * turn, 1), out)
        return out[0:1]

    same_row = ((r0 >> 2) & 3) == (r1 >> 5)
    wanted = ((r0 >> 4) * SLOTS + (r0 & 3)).astype(F32)
    forward = onehot(same_row & (tiled(code) == wanted))
    forward_over = onehot(same_row & (tiled(code_over) == wanted))
    code_col = jnp.sum(
        jnp.where(r1 == (r0 & 31), jnp.broadcast_to(code, (128, 128)), 0.0), axis=1, keepdims=True
    )
    code_col = jnp.where((r0[:, 0:1] & 31) < MROW, code_col, -1.0)
    b0, b1 = iota((128, 512), 0), iota((128, 512), 1)
    whose = ((b0 >> 5) == ((b1 >> 2) & 3)) & (code_col == (b1 >> 4).astype(F32))
    back = [onehot(whose & ((b1 & 3) == q)) for q in range(4)]
    e0, e1 = iota((256, 128), 0), iota((256, 128), 1)
    mine = (place[0:1] == (e0 >> 5).astype(F32)) & (plane_row == z_here.astype(F32))
    pick = jnp.sum(jnp.where(mine, rank + 1.0, 0.0), axis=1, keepdims=True) - 1.0
    match = (((e0 >> 2) & 7) == (e1 >> 4)) & ((e0 & 3) == ((e1 >> 2) & 3))
    slot = (e1 & 3).astype(F32)
    give = onehot(match & (pick == slot))
    give_over = onehot(match & (pick == slot + SLOTS))
    return forward, forward_over, back, give, give_over


def kernel(
    grads_hbm,
    momentum_hbm,
    owners_ref,
    newm_hbm,
    update_hbm,
    owned_hbm,
    newm_ref,
    update_ref,
    owned_ref,
    grads,
    momentum,
    s_direct,
    s_far,
    s_comb,
    r_direct,
    r_far,
    r_comb,
    part,
    own,
    nest,
    zs_f,
    zr_f,
    zs_o,
    zr_o,
    zs_r,
    zr_r,
    ys_p,
    x_p,
    x_d,
    ys_o,
    x_o,
    x_a,
    x_b,
    gram_f,
    gram_b,
    poly_b,
    m_forward,
    m_over,
    m_back,
    m_give,
    m_give_over,
    load_sem,
    store_sem,
    x_send,
    direct_sem,
    far_sem,
    comb_sem,
    z_send,
    zf_sem,
    zo_sem,
    r_send,
    zr_sem,
    y_send,
    yp_sem,
    yo_sem,
    all_in,
):
    x = lax.axis_index("dp")
    here = lax.axis_index("shard")
    y, z, c = here // 16, (here // 2) % NZ, here % 2
    e = 2 * y + c
    right, left, far = (x + 1) % NX, (x + 3) % NX, (x + 2) % NX

    def at(y_, z_, c_):
        return (x, (y_ * NZ + z_) * 2 + c_)

    def send(src, dst, send_sem, recv_sem, device):
        pltpu.make_async_remote_copy(
            src_ref=src, dst_ref=dst, send_sem=send_sem, recv_sem=recv_sem,
            device_id=device, device_id_type=MESH,
        ).start()

    def wait_recv(ref, sem):
        pltpu.make_async_remote_copy(
            src_ref=ref, dst_ref=ref, send_sem=sem, recv_sem=sem,
            device_id=(x, here), device_id_type=MESH,
        ).wait_recv()

    def wait_send(ref, sem):
        pltpu.make_async_remote_copy(
            src_ref=ref, dst_ref=ref, send_sem=sem, recv_sem=sem,
            device_id=(x, here), device_id_type=MESH,
        ).wait_send()

    def load(k):
        return pltpu.make_async_copy(
            grads_hbm.at[:, :, pl.ds(k * WIDE, WIDE)], grads.at[k], load_sem.at[k]
        )

    load_momentum = pltpu.make_async_copy(momentum_hbm, momentum, load_sem.at[CHUNKS])
    for k in range(CHUNKS):
        load(k).start()
    load_momentum.start()

    def store(i, k):
        src, dst = ((newm_ref, newm_hbm), (update_ref, update_hbm))[i]
        cols = pl.ds(k * WIDE, WIDE)
        return pltpu.make_async_copy(src.at[:, :, cols], dst.at[:, :, cols], store_sem.at[i, k])

    store_owned = pltpu.make_async_copy(owned_ref, owned_hbm, store_sem.at[2, 0])

    barrier = pltpu.get_barrier_semaphore()
    for device in ((right, here), (left, here)):
        pl.semaphore_signal(barrier, 1, device_id=device, device_id_type=MESH)
    for step in range(1, NZ):
        pl.semaphore_signal(barrier, 1, device_id=at(y, (z + step) % NZ, c), device_id_type=MESH)
    for step in range(1, 8):
        other = (e + step) % 8
        pl.semaphore_signal(
            barrier, 1, device_id=at(other // 2, z, other % 2), device_id_type=MESH
        )

    owner = jnp.concatenate([owners_ref[...], jnp.zeros((1, 16), I32)], axis=1)
    owner = pltpu.roll(jnp.broadcast_to(owner, (8, 128)), (128 - MROW * x) % 128, 1)
    forward, forward_over, back, give, give_over = routes(owner, z)
    m_forward[...] = forward
    m_over[...] = forward_over
    for q in range(4):
        m_back[128 * q : 128 * (q + 1)] = back[q]
    m_give[...] = give
    m_give_over[...] = give_over
    nest[...] = jnp.zeros_like(nest)

    p0, p1 = iota((112, 128), 0), iota((112, 128), 1)
    quarter = (
        jnp.where(p0 >= 28, 1, 0) + jnp.where(p0 >= 56, 1, 0) + jnp.where(p0 >= 84, 1, 0)
    )

    def packing(parity):
        return onehot(p1 == p0 + 4 * quarter + 4 * parity)

    def window(k, to, table, g):
        start = pl.multiple_of(((MROW * to) // 8) * 8, 8)
        rows = grads[k, 4 * g : 4 * g + 4, pl.ds(start, 32), :].astype(BF).reshape(128, WIDE)
        return dot(table, rows)

    def pack(k):
        load(k).wait()
        odd = packing((x + 1) % 2)
        even = packing(x % 2)
        for g in range(3):
            v = window(k, far, even, g).astype(BF)
            s_far[0, k, g] = v[:, :HALF]
            s_far[1, k, g] = v[:, HALF:]
            v = window(k, right, odd, g)
            part[0, k, g] = v[:, :HALF]
            s_direct[0, k, g] = v[:, HALF:].astype(BF)
            v = window(k, left, odd, g)
            part[1, k, g] = v[:, HALF:]
            s_direct[1, k, g] = v[:, :HALF].astype(BF)

    def pack_own(k):
        even = packing(x % 2)
        for g in range(3):
            own[k, g] = window(k, x, even, g)

    towards = ((right, here), (left, here))

    def send_first(k):
        for way in range(2):
            send(s_far.at[way, k], r_far.at[way, k], x_send.at[0], far_sem.at[way, k], towards[way])
        for way in range(2):
            send(
                s_direct.at[way, k], r_direct.at[way, k], x_send.at[1], direct_sem.at[way, k],
                towards[way],
            )

    def send_combined(k):
        for way in range(2):
            wait_recv(r_far.at[way, k], far_sem.at[way, k])
            s_comb[way, k] = (part[way, k] + r_far[way, k].astype(F32)).astype(BF)
            send(
                s_comb.at[way, k], r_comb.at[way, k], x_send.at[2], comb_sem.at[way, k],
                towards[way],
            )

    def gradient(k):
        for way in range(2):
            wait_recv(r_direct.at[way, k], direct_sem.at[way, k])
            wait_recv(r_comb.at[way, k], comb_sem.at[way, k])
        low = own[k, :, :, :HALF] + r_direct[1, k].astype(F32) + r_comb[0, k].astype(F32)
        high = own[k, :, :, HALF:] + r_direct[0, k].astype(F32) + r_comb[1, k].astype(F32)
        own[k, :, :, :HALF] = low
        own[k, :, :, HALF:] = high
        for g in range(3):
            for rr in range(4):
                total = own[k, g, MROW * rr : MROW * (rr + 1), :]
                cols = slice(k * WIDE, (k + 1) * WIDE)
                moved = momentum_decay * momentum[4 * g + rr, :, cols] + total
                newm_ref[4 * g + rr, :, cols] = moved
                nest[g, 32 * rr : 32 * rr + MROW, :] = total + momentum_decay * moved
        store(0, k).start()

    def send_z(zs, zr, k, sem, recv_sem):
        zr[k, pl.ds(z, 1)] = zs[k, pl.ds(z, 1)]
        for step in (1, 7, 2, 6, 3, 5, 4):
            to = (z + step) % NZ
            send(zs.at[k, to], zr.at[k, z], sem, recv_sem.at[k], at(y, to, c))

    def forward_z(k):
        for g in range(3):
            rows = nest[g].astype(BF)
            zs_f[k, :, g] = dot(m_forward[...], rows).astype(BF).reshape(NZ, 16, WIDE)
        send_z(zs_f, zr_f, k, z_send.at[0], zf_sem)
        for g in range(3):
            rows = nest[g].astype(BF)
            zs_o[k, :, g] = dot(m_over[...], rows).astype(BF).reshape(NZ, 16, WIDE)

    def forward_over_z(k):
        send_z(zs_o, zr_o, k, z_send.at[1], zo_sem)

    i0, i1 = iota((128, 128), 0), iota((128, 128), 1)
    to_slots = lambda: onehot(i1 == ((i0 & 31) << 2) + (i0 >> 5))
    from_slots = lambda: onehot(i0 == ((i1 & 31) << 2) + (i1 >> 5))

    def others(n, me):
        return [(me + step) % n for step in range(1, n)]

    def relay_p(k):
        wait_recv(zr_f.at[k, pl.ds(0, 7)], zf_sem.at[k])
        table = to_slots()
        for g in range(3):
            rows = zr_f[k, :, g].reshape(128, WIDE)
            ys_p[k, :, g] = dot(table, rows).astype(BF).reshape(SLOTS, 32, WIDE)
        for to in others(NY, y):
            send(ys_p.at[k, to], x_p.at[k, e], y_send.at[0], yp_sem.at[k], at(to, z, 0))

        @pl.when(c == 0)
        def _():
            x_p[k, pl.ds(e, 1)] = ys_p[k, pl.ds(y, 1)]

        @pl.when(c == 1)
        def _():
            send(ys_p.at[k, y], x_p.at[k, e], y_send.at[1], yp_sem.at[k], at(y, z, 0))

    def matrix(ref, k):
        return ref[k].reshape(F, WIDE)

    blocks = [(i, j) for i in range(3) for j in range(i, 3)]

    def block(ref, i, j):
        return ref.at[256 * i : 256 * (i + 1), 256 * j : 256 * (j + 1)]

    def add_gram(src, k):
        rows = matrix(src, k)
        for i, j in blocks:
            new = dot_t(rows[256 * i : 256 * (i + 1)], rows[256 * j : 256 * (j + 1)])
            into = block(gram_f, i, j)
            into[...] = new if k == 0 else into[...] + new

    def put_gram(i, j, value):
        value = value.astype(BF)
        block(gram_b, i, j)[...] = value
        if i != j:
            block(gram_b, j, i)[...] = value.T

    def whole_gram(src):
        for i, j in blocks:
            total = 0.0
            for k in range(CHUNKS):
                rows = matrix(src, k)
                total = total + dot_t(
                    rows[256 * i : 256 * (i + 1)], rows[256 * j : 256 * (j + 1)]
                )
            put_gram(i, j, total)

    def poly():
        for i, j in blocks:
            square = dot(
                gram_b[256 * i : 256 * (i + 1), :], gram_b[:, 256 * j : 256 * (j + 1)]
            )
            value = coeff_second * block(gram_b, i, j)[...].astype(F32) + coeff_third * square
            value = value.astype(BF)
            block(poly_b, i, j)[...] = value
            if i != j:
                block(poly_b, j, i)[...] = value.T

    def advance(src, dst, k):
        rows = matrix(src, k)
        out = coeff_first * rows.astype(F32) + dot(poly_b[...], rows)
        dst[k] = out.astype(BF).reshape(8, 3, 32, WIDE)

    def finish(src, dst, done, between):
        d0, d1 = iota((256, 256), 0), iota((256, 256), 1)
        squares = 0.0
        for i in range(3):
            squares = squares + jnp.sum(jnp.where(d0 == d1, block(gram_f, i, i)[...], 0.0))
        inverse = 1.0 / (jnp.sqrt(squares) + epsilon_norm)
        for i, j in blocks:
            put_gram(i, j, block(gram_f, i, j)[...] * (inverse * inverse))
        for k in range(CHUNKS):
            x_a[k] = (src[k].astype(F32) * inverse).astype(BF)
        poly()
        for k in range(CHUNKS):
            advance(x_a, x_b, k)
        between()
        whole_gram(x_b)
        poly()
        for k in range(CHUNKS):
            advance(x_b, dst, k)
            done(k)

    def send_back(k):
        if k % 2 == 0:
            return
        half = k // 2
        table = from_slots()

        @pl.loop(0, 8)
        def _(step):
            to = (e + step) % 8
            rows = jnp.concatenate(
                [
                    jnp.concatenate(
                        [
                            x_d[k - 1 + q // 2, to, g, :, NARROW * (q % 2) : NARROW * (q % 2 + 1)]
                            for g in range(3)
                        ],
                        axis=1,
                    )
                    for q in range(4)
                ],
                axis=0,
            )
            rows = dot(table, rows).astype(BF).reshape(NZ, 16, 3 * NARROW)
            zs_r[half, pl.ds(to * NZ, NZ)] = rows

            for near in (0, 1, 7, 2, 6, 3, 5, 4):
                to_z = (z + near) % NZ

                def give():
                    send(
                        zs_r.at[half, to * NZ + to_z], zr_r.at[half, z * SLOTS + y], r_send,
                        zr_sem.at[half], at(to // 2, to_z, to % 2),
                    )

                if near == 0:

                    @pl.when(step > 0)
                    def _():
                        give()
                else:
                    give()

        zr_r[half, pl.ds(z * SLOTS + y, 1)] = zs_r[half, pl.ds(e * NZ + z, 1)]

    def primary_gram(k):
        @pl.when(c == 0)
        def _():
            wait_recv(x_p.at[k, pl.ds(0, 7)], yp_sem.at[k])
            add_gram(x_p, k)

    def relay_o(k):
        wait_recv(zr_o.at[k, pl.ds(0, 7)], zo_sem.at[k])
        for g in range(3):
            rows = dot(m_give[...], zr_f[k, :, g].reshape(128, WIDE)) + dot(
                m_give_over[...], zr_o[k, :, g].reshape(128, WIDE)
            )
            ys_o[k, :, g] = rows.astype(BF).reshape(8, 32, WIDE)
        x_o[k, pl.ds(e, 1)] = ys_o[k, pl.ds(e, 1)]
        for to in others(8, e):
            send(ys_o.at[k, to], x_o.at[k, e], y_send.at[2], yo_sem.at[k], at(to // 2, z, to % 2))

    def owner_part():
        for k in range(CHUNKS):
            wait_recv(x_o.at[k, pl.ds(0, 7)], yo_sem.at[k])
            add_gram(x_o, k)

        t0, t1 = iota((192, 192), 0), iota((192, 192), 1)
        g0 = jnp.where((t1 % 96) >= 64, 2, jnp.where((t1 % 96) >= 32, 1, 0))
        c0 = jnp.where(t1 >= 96, 1, 0)
        place = ((t1 >> 2) & 7) * 24 + c0 * 12 + g0 * 4 + (t1 & 3)
        table = onehot(t0 == place)

        def done(k):
            for b in range(4):
                rows = x_a[k, 2 * b : 2 * b + 2].reshape(192, WIDE)
                owned_ref[192 * b : 192 * (b + 1), k * WIDE : (k + 1) * WIDE] = dot(
                    table, rows
                ).astype(BF)

        finish(x_o, x_a, done, lambda: None)
        store_owned.start()

    def unpack(half):
        @pl.when(c == 0)
        def _():
            wait_recv(zr_r.at[half, pl.ds(0, 31)], zr_sem.at[half])

        @pl.when(c == 1)
        def _():
            wait_recv(zr_r.at[half, pl.ds(0, 32)], zr_sem.at[half])

        for q in range(4):
            rows = zr_r[half].reshape(512, 3 * NARROW)
            rows = dot(m_back[128 * q : 128 * (q + 1)], rows) * SCALE
            for g in range(3):
                for rr in range(4):
                    first = 512 * half + NARROW * q
                    update_ref[4 * g + rr, :, first : first + NARROW] = rows[
                        32 * rr : 32 * rr + MROW, NARROW * g : NARROW * (g + 1)
                    ]
        for k in (2 * half, 2 * half + 1):
            store(1, k).start()

    pack(0)
    pl.semaphore_wait(barrier, 16)
    for step in range(1, NZ):
        pl.semaphore_signal(all_in, 1, device_id=at(y, (z + step) % NZ, c), device_id_type=MESH)
    send_first(0)
    pack(1)
    send_first(1)
    send_combined(0)
    pack(2)
    send_first(2)
    pack_own(0)
    load_momentum.wait()
    for k in range(CHUNKS):
        if k + 1 < CHUNKS:
            send_combined(k + 1)
        if k + 3 < CHUNKS:
            pack(k + 3)
            send_first(k + 3)
        if k + 1 < CHUNKS:
            pack_own(k + 1)
        gradient(k)
        forward_z(k)
        if k >= 1:
            relay_p(k - 1)
        if k >= 2:
            primary_gram(k - 2)
    forward_over_z(0)
    forward_over_z(1)
    relay_p(CHUNKS - 1)
    forward_over_z(2)
    forward_over_z(3)
    primary_gram(CHUNKS - 2)
    primary_gram(CHUNKS - 1)
    pl.semaphore_wait(all_in, NZ - 1)

    @pl.when(c == 0)
    def _():
        def between():
            relay_o(0)
            relay_o(1)

        finish(x_p, x_d, send_back, between)

    @pl.when(c == 1)
    def _():
        relay_o(0)
        relay_o(1)

    relay_o(2)
    relay_o(3)
    owner_part()
    for half in range(2):
        unpack(half)
    for k in range(CHUNKS):
        store(0, k).wait()
        store(1, k).wait()
    store_owned.wait()

    wait_send(s_far, x_send.at[0])
    wait_send(s_direct, x_send.at[1])
    wait_send(s_comb, x_send.at[2])
    for i, ref in enumerate((zs_f, zs_o)):
        wait_send(ref.at[:, pl.ds(0, 7)], z_send.at[i])
    wait_send(ys_p.at[:, pl.ds(0, 3)], y_send.at[0])

    @pl.when(c == 1)
    def _():
        wait_send(ys_p.at[:, 0], y_send.at[1])

    @pl.when(c == 0)
    def _():
        wait_send(zs_r.at[:, pl.ds(0, 63)], r_send)

    wait_send(ys_o.at[:, pl.ds(0, 7)], y_send.at[2])


def scratch():
    def vmem(*shape, dtype=BF):
        return pltpu.VMEM(shape, dtype)

    dma = pltpu.SemaphoreType.DMA
    x_half = (2, CHUNKS, 3, 112, HALF)
    z_all = (CHUNKS, NZ, 3, 16, WIDE)
    plane = (CHUNKS, 8, 3, 32, WIDE)
    quarter = (CHUNKS, SLOTS, 3, 32, WIDE)
    return [
        vmem(12, MROW, D, dtype=F32),
        vmem(12, MROW, D, dtype=F32),
        vmem(F, D),
        vmem(CHUNKS, 12, 112, WIDE, dtype=F32),
        vmem(12, MROW, D, dtype=F32),
        *[vmem(*x_half) for _ in range(6)],
        vmem(*x_half, dtype=F32),
        vmem(CHUNKS, 3, 112, WIDE, dtype=F32),
        vmem(3, 128, WIDE, dtype=F32),
        *[vmem(*z_all) for _ in range(4)],
        vmem(2, 64, 16, 3 * NARROW),
        vmem(2, 32, 16, 3 * NARROW),
        vmem(*quarter),
        vmem(*plane),
        vmem(*plane),
        vmem(*plane),
        vmem(*plane),
        vmem(*plane),
        vmem(*plane),
        vmem(F, F, dtype=F32),
        vmem(F, F),
        vmem(F, F),
        vmem(128, 128),
        vmem(128, 128),
        vmem(512, 512),
        vmem(256, 128),
        vmem(256, 128),
        dma((CHUNKS + 1,)),
        dma((3, CHUNKS)),
        dma((3,)),
        dma((2, CHUNKS)),
        dma((2, CHUNKS)),
        dma((2, CHUNKS)),
        dma((2,)),
        dma((CHUNKS,)),
        dma((CHUNKS,)),
        dma(()),
        dma((2,)),
        dma((3,)),
        dma((CHUNKS,)),
        dma((CHUNKS,)),
        pltpu.SemaphoreType.REGULAR,
    ]


def hand_over(*refs):
    srcs, dsts, held = refs[:3], refs[3:6], refs[6:9]
    in_sem, out_sem = refs[9:]

    def move(i, piece, src, dst, sem):
        rows = src.shape[0] // PIECES
        part = pl.ds(piece * rows, rows)
        return pltpu.make_async_copy(src.at[part], dst.at[part], sem.at[i, piece])

    each = [(i, piece) for i in range(3) for piece in range(PIECES)]
    for i, piece in each:
        move(i, piece, srcs[i], held[i], in_sem).start()
    for i, piece in each:
        move(i, piece, srcs[i], held[i], in_sem).wait()
        move(i, piece, held[i], dsts[i], out_sem).start()
    for i, piece in each:
        move(i, piece, held[i], dsts[i], out_sem).wait()


def local(partial_grads, momentum, owners):
    grads = jnp.transpose(partial_grads[0], (1, 0, 2))
    held = jnp.transpose(momentum, (1, 0, 2))
    owners = owners.reshape(1, 112)
    vmem = pl.BlockSpec(memory_space=pltpu.VMEM)
    anywhere = pl.BlockSpec(memory_space=pl.ANY)
    outs = (
        jax.ShapeDtypeStruct((12, MROW, D), F32),
        jax.ShapeDtypeStruct((12, MROW, D), F32),
        jax.ShapeDtypeStruct((F, D), BF),
    )
    results = pl.pallas_call(
        kernel,
        out_shape=outs,
        in_specs=[anywhere, anywhere, vmem],
        out_specs=(anywhere,) * 3,
        scratch_shapes=scratch(),
        compiler_params=pltpu.CompilerParams(
            collective_id=0, has_side_effects=True, vmem_limit_bytes=60 << 20
        ),
    )(grads, held, owners)
    new_momentum, update, owned = pl.pallas_call(
        hand_over,
        out_shape=outs,
        in_specs=[anywhere] * 3,
        out_specs=(anywhere,) * 3,
        scratch_shapes=[pltpu.VMEM(out.shape, out.dtype) for out in outs]
        + [pltpu.SemaphoreType.DMA((3, PIECES))] * 2,
        compiler_params=pltpu.CompilerParams(vmem_limit_bytes=60 << 20),
    )(*results)
    return (
        jnp.transpose(new_momentum, (1, 0, 2)),
        jnp.transpose(update, (1, 0, 2)),
        owned[None, None],
    )


def solution(mesh):
    return jax.shard_map(
        local,
        mesh=mesh,
        in_specs=(P("dp", None, "shard", None), P("dp", "shard", None), P()),
        out_specs=(P("dp", "shard", None), P("dp", "shard", None), P("dp", "shard", None, None)),
        check_vma=False,
    )
```

```python
import functools
import math

import jax
import jax.numpy as jnp
from jax import lax
from jax.experimental import pallas as pl
from jax.experimental.pallas import tpu as pltpu
from jax.sharding import PartitionSpec as P


MESH = pl.DeviceIdType.MESH
BF = jnp.bfloat16
F32 = jnp.float32
I32 = jnp.int32

D, F = 1024, 768
NX, NY, NZ = 4, 4, 8
MROW = 28
CHUNKS, WIDE = 4, 256
HALF = NARROW = WIDE // 2
SLOTS = 4
PIECES = 4
SCALE = 0.2 * math.sqrt(max(F, D))

momentum_decay = 0.95
epsilon_norm = 1e-07
coeff_first = 3.4445
coeff_second = -4.775
coeff_third = 2.0315


def iota(shape, axis):
    return lax.broadcasted_iota(I32, shape, axis)


def onehot(cond):
    return jnp.where(cond, 1.0, 0.0).astype(BF)


def dot(a, b):
    return jnp.dot(a, b, preferred_element_type=F32)


def dot_t(a, b):
    return lax.dot_general(a, b, (((1,), (1,)), ((), ())), preferred_element_type=F32)


def routes(owner, chip_here):
    r0, r1 = iota((128, 128), 0), iota((128, 128), 1)
    owner = jnp.broadcast_to(owner[0:1], (128, 128))
    valid = r1 < MROW
    chip = jnp.where(valid, ((owner >> 1) & 7) * SLOTS + (owner >> 4), -1).astype(F32)
    core = jnp.where(valid, owner & 1, -1)
    first, second = core == 0, core == 1
    diag, before = r0 == r1, r0 < r1
    r0f = r0.astype(F32)

    def over_rows(cond, value=1.0):
        return jnp.sum(jnp.where(cond, value, 0.0), axis=0, keepdims=True)

    def over_lanes(cond, value=1.0):
        return jnp.sum(jnp.where(cond, value, 0.0), axis=1, keepdims=True)

    second_col = over_lanes(diag & second)
    nth = over_rows(before & (second_col > 0.5))
    taken = over_lanes(first & (chip == r0f))
    free = jnp.where((r0[:, 0:1] < NZ * SLOTS) & (taken < 0.5), 1.0, 0.0)
    free_row = over_rows(diag & (free > 0.5))
    free_before = over_lanes((r1 < r0) & (free_row > 0.5))
    away = over_rows((free > 0.5) & (free_before == nth), r0f)
    first, second, valid, chip = first[0:1], second[0:1], valid[0:1], chip[0:1]
    code = jnp.where(first, chip, jnp.where(second, away, -1.0))
    code_over = jnp.where(second, chip, -1.0)
    owns = jnp.sum(
        jnp.where(first & (chip == chip_here.astype(F32)), 1.0, 0.0), axis=1, keepdims=True
    )

    def tiled(row):
        row = jnp.where(valid, row, -1.0)
        wide = jnp.broadcast_to(row, (8, 128))
        out = wide
        for turn in (1, 2, 3):
            lane = iota((8, 128), 1)
            out = jnp.where((lane >> 5) == turn, pltpu.roll(wide, 32 * turn, 1), out)
        return out[0:1]

    same_row = ((r0 >> 2) & 3) == (r1 >> 5)
    wanted = ((r0 >> 4) * SLOTS + (r0 & 3)).astype(F32)
    forward = onehot(same_row & (tiled(code) == wanted))
    forward_over = onehot(same_row & (tiled(code_over) == wanted))
    code_col = jnp.sum(
        jnp.where(r1 == (r0 & 31), jnp.broadcast_to(code, (128, 128)), 0.0), axis=1, keepdims=True
    )
    code_col = jnp.where((r0[:, 0:1] & 31) < MROW, code_col, -1.0)
    b0, b1 = iota((128, 512), 0), iota((128, 512), 1)
    whose = ((b0 >> 5) == ((b1 >> 2) & 3)) & (code_col == (b1 >> 4).astype(F32))
    back = [onehot(whose & ((b1 & 3) == q)) for q in range(4)]
    return forward, forward_over, back, owns


def kernel(
    grads_hbm,
    momentum_hbm,
    owners_ref,
    newm_hbm,
    update_hbm,
    owned_hbm,
    newm_ref,
    update_ref,
    owned_ref,
    grads,
    momentum,
    s_direct,
    s_far,
    s_comb,
    r_direct,
    r_far,
    r_comb,
    part,
    own,
    nest,
    zs_f,
    zr_f,
    zs_o,
    zr_o,
    zs_r,
    zr_r,
    ys_p,
    x_in,
    x_d,
    ys_o,
    x_a,
    x_b,
    gram_f,
    gram_b,
    poly_b,
    m_forward,
    m_over,
    m_back,
    m_owns,
    load_sem,
    store_sem,
    x_send,
    direct_sem,
    far_sem,
    comb_sem,
    z_send,
    zf_sem,
    zo_sem,
    r_send,
    zr_sem,
    y_send,
    in_sem,
    all_in,
):
    x = lax.axis_index("dp")
    here = lax.axis_index("shard")
    y, z, c = here // 16, (here // 2) % NZ, here % 2
    e = 2 * y + c
    right, left, far = (x + 1) % NX, (x + 3) % NX, (x + 2) % NX

    def at(y_, z_, c_):
        return (x, (y_ * NZ + z_) * 2 + c_)

    def send(src, dst, send_sem, recv_sem, device):
        pltpu.make_async_remote_copy(
            src_ref=src, dst_ref=dst, send_sem=send_sem, recv_sem=recv_sem,
            device_id=device, device_id_type=MESH,
        ).start()

    def wait_recv(ref, sem):
        pltpu.make_async_remote_copy(
            src_ref=ref, dst_ref=ref, send_sem=sem, recv_sem=sem,
            device_id=(x, here), device_id_type=MESH,
        ).wait_recv()

    def wait_send(ref, sem):
        pltpu.make_async_remote_copy(
            src_ref=ref, dst_ref=ref, send_sem=sem, recv_sem=sem,
            device_id=(x, here), device_id_type=MESH,
        ).wait_send()

    def load(k):
        return pltpu.make_async_copy(
            grads_hbm.at[:, :, pl.ds(k * WIDE, WIDE)], grads.at[k], load_sem.at[k]
        )

    load_momentum = pltpu.make_async_copy(momentum_hbm, momentum, load_sem.at[CHUNKS])
    for k in range(CHUNKS):
        load(k).start()
    load_momentum.start()

    def store(i, k):
        src, dst = ((newm_ref, newm_hbm), (update_ref, update_hbm))[i]
        cols = pl.ds(k * WIDE, WIDE)
        return pltpu.make_async_copy(src.at[:, :, cols], dst.at[:, :, cols], store_sem.at[i, k])

    store_owned = pltpu.make_async_copy(owned_ref, owned_hbm, store_sem.at[2, 0])

    barrier = pltpu.get_barrier_semaphore()
    for device in ((right, here), (left, here)):
        pl.semaphore_signal(barrier, 1, device_id=device, device_id_type=MESH)
    for step in range(1, NZ):
        pl.semaphore_signal(barrier, 1, device_id=at(y, (z + step) % NZ, c), device_id_type=MESH)
    for step in range(1, 8):
        other = (e + step) % 8
        pl.semaphore_signal(
            barrier, 1, device_id=at(other // 2, z, other % 2), device_id_type=MESH
        )

    owner = jnp.concatenate([owners_ref[...], jnp.zeros((1, 16), I32)], axis=1)
    owner = pltpu.roll(jnp.broadcast_to(owner, (8, 128)), (128 - MROW * x) % 128, 1)
    forward, forward_over, back, owns = routes(owner, z * SLOTS + y)
    m_forward[...] = forward
    m_over[...] = forward_over
    for q in range(4):
        m_back[128 * q : 128 * (q + 1)] = back[q]
    m_owns[...] = jnp.broadcast_to(owns, (8, 128))
    nest[...] = jnp.zeros_like(nest)

    p0, p1 = iota((112, 128), 0), iota((112, 128), 1)
    quarter = (
        jnp.where(p0 >= 28, 1, 0) + jnp.where(p0 >= 56, 1, 0) + jnp.where(p0 >= 84, 1, 0)
    )

    def packing(parity):
        return onehot(p1 == p0 + 4 * quarter + 4 * parity)

    def window(k, to, table, g):
        start = pl.multiple_of(((MROW * to) // 8) * 8, 8)
        rows = grads[k, 4 * g : 4 * g + 4, pl.ds(start, 32), :].astype(BF).reshape(128, WIDE)
        return dot(table, rows)

    def pack(k):
        load(k).wait()
        odd = packing((x + 1) % 2)
        even = packing(x % 2)
        for g in range(3):
            v = window(k, far, even, g).astype(BF)
            s_far[0, k, g] = v[:, :HALF]
            s_far[1, k, g] = v[:, HALF:]
            v = window(k, right, odd, g)
            part[0, k, g] = v[:, :HALF]
            s_direct[0, k, g] = v[:, HALF:].astype(BF)
            v = window(k, left, odd, g)
            part[1, k, g] = v[:, HALF:]
            s_direct[1, k, g] = v[:, :HALF].astype(BF)

    def pack_own(k):
        even = packing(x % 2)
        for g in range(3):
            own[k, g] = window(k, x, even, g)

    towards = ((right, here), (left, here))

    def send_first(k):
        for way in range(2):
            send(s_far.at[way, k], r_far.at[way, k], x_send.at[0], far_sem.at[way, k], towards[way])
        for way in range(2):
            send(
                s_direct.at[way, k], r_direct.at[way, k], x_send.at[1], direct_sem.at[way, k],
                towards[way],
            )

    def send_combined(k):
        for way in range(2):
            wait_recv(r_far.at[way, k], far_sem.at[way, k])
            s_comb[way, k] = (part[way, k] + r_far[way, k].astype(F32)).astype(BF)
            send(
                s_comb.at[way, k], r_comb.at[way, k], x_send.at[2], comb_sem.at[way, k],
                towards[way],
            )

    def gradient(k):
        for way in range(2):
            wait_recv(r_direct.at[way, k], direct_sem.at[way, k])
            wait_recv(r_comb.at[way, k], comb_sem.at[way, k])
        low = own[k, :, :, :HALF] + r_direct[1, k].astype(F32) + r_comb[0, k].astype(F32)
        high = own[k, :, :, HALF:] + r_direct[0, k].astype(F32) + r_comb[1, k].astype(F32)
        own[k, :, :, :HALF] = low
        own[k, :, :, HALF:] = high
        for g in range(3):
            for rr in range(4):
                total = own[k, g, MROW * rr : MROW * (rr + 1), :]
                cols = slice(k * WIDE, (k + 1) * WIDE)
                moved = momentum_decay * momentum[4 * g + rr, :, cols] + total
                newm_ref[4 * g + rr, :, cols] = moved
                nest[g, 32 * rr : 32 * rr + MROW, :] = total + momentum_decay * moved
        store(0, k).start()

    def send_z(zs, zr, k, sem, recv_sem):
        zr[k, pl.ds(z, 1)] = zs[k, pl.ds(z, 1)]
        for step in (1, 7, 2, 6, 3, 5, 4):
            to = (z + step) % NZ
            send(zs.at[k, to], zr.at[k, z], sem, recv_sem.at[k], at(y, to, c))

    def forward_z(k):
        for g in range(3):
            rows = nest[g].astype(BF)
            zs_f[k, :, g] = dot(m_forward[...], rows).astype(BF).reshape(NZ, 16, WIDE)
        send_z(zs_f, zr_f, k, z_send.at[0], zf_sem)
        for g in range(3):
            rows = nest[g].astype(BF)
            zs_o[k, :, g] = dot(m_over[...], rows).astype(BF).reshape(NZ, 16, WIDE)

    def forward_over_z(k):
        send_z(zs_o, zr_o, k, z_send.at[1], zo_sem)

    i0, i1 = iota((128, 128), 0), iota((128, 128), 1)
    to_slots = lambda: onehot(i1 == ((i0 & 31) << 2) + (i0 >> 5))
    from_slots = lambda: onehot(i0 == ((i1 & 31) << 2) + (i1 >> 5))

    def others(n, me):
        return [(me + step) % n for step in range(1, n)]

    def relay(k, zr, ys, sem, core):
        table = to_slots()
        for g in range(3):
            rows = zr[k, :, g].reshape(128, WIDE)
            ys[k, :, g] = dot(table, rows).astype(BF).reshape(SLOTS, 32, WIDE)
        for to in others(NY, y):
            send(ys.at[k, to], x_in.at[k, e], y_send.at[sem], in_sem.at[k], at(to, z, core))

        @pl.when(c == core)
        def _():
            x_in[k, pl.ds(e, 1)] = ys[k, pl.ds(y, 1)]

        @pl.when(c != core)
        def _():
            send(ys.at[k, y], x_in.at[k, e], y_send.at[sem + 1], in_sem.at[k], at(y, z, core))

    def relay_p(k):
        wait_recv(zr_f.at[k, pl.ds(0, 7)], zf_sem.at[k])
        relay(k, zr_f, ys_p, 0, 0)

    def relay_o(k):
        wait_recv(zr_o.at[k, pl.ds(0, 7)], zo_sem.at[k])
        relay(k, zr_o, ys_o, 2, 1)

    def matrix(ref, k):
        return ref[k].reshape(F, WIDE)

    blocks = [(i, j) for i in range(3) for j in range(i, 3)]

    def block(ref, i, j):
        return ref.at[256 * i : 256 * (i + 1), 256 * j : 256 * (j + 1)]

    def add_gram(src, k):
        rows = matrix(src, k)
        for i, j in blocks:
            new = dot_t(rows[256 * i : 256 * (i + 1)], rows[256 * j : 256 * (j + 1)])
            into = block(gram_f, i, j)
            into[...] = new if k == 0 else into[...] + new

    def put_gram(i, j, value):
        value = value.astype(BF)
        block(gram_b, i, j)[...] = value
        if i != j:
            block(gram_b, j, i)[...] = value.T

    def whole_gram(src):
        for i, j in blocks:
            total = 0.0
            for k in range(CHUNKS):
                rows = matrix(src, k)
                total = total + dot_t(
                    rows[256 * i : 256 * (i + 1)], rows[256 * j : 256 * (j + 1)]
                )
            put_gram(i, j, total)

    def poly():
        for i, j in blocks:
            square = dot(
                gram_b[256 * i : 256 * (i + 1), :], gram_b[:, 256 * j : 256 * (j + 1)]
            )
            value = coeff_second * block(gram_b, i, j)[...].astype(F32) + coeff_third * square
            value = value.astype(BF)
            block(poly_b, i, j)[...] = value
            if i != j:
                block(poly_b, j, i)[...] = value.T

    def advance(src, dst, k):
        rows = matrix(src, k)
        out = coeff_first * rows.astype(F32) + dot(poly_b[...], rows)
        dst[k] = out.astype(BF).reshape(8, 3, 32, WIDE)

    def finish(src, dst, done, between):
        d0, d1 = iota((256, 256), 0), iota((256, 256), 1)
        squares = 0.0
        for i in range(3):
            squares = squares + jnp.sum(jnp.where(d0 == d1, block(gram_f, i, i)[...], 0.0))
        inverse = 1.0 / (jnp.sqrt(squares) + epsilon_norm)
        for i, j in blocks:
            put_gram(i, j, block(gram_f, i, j)[...] * (inverse * inverse))
        for k in range(CHUNKS):
            x_a[k] = (src[k].astype(F32) * inverse).astype(BF)
        poly()
        for k in range(CHUNKS):
            advance(x_a, x_b, k)
        between()
        whole_gram(x_b)
        poly()
        for k in range(CHUNKS):
            advance(x_b, dst, k)
            done(k)

    def send_back(k):
        if k % 2 == 0:
            return
        half = k // 2
        table = from_slots()

        @pl.loop(0, 8)
        def _(step):
            to = (e + step) % 8
            rows = jnp.concatenate(
                [
                    jnp.concatenate(
                        [
                            x_d[k - 1 + q // 2, to, g, :, NARROW * (q % 2) : NARROW * (q % 2 + 1)]
                            for g in range(3)
                        ],
                        axis=1,
                    )
                    for q in range(4)
                ],
                axis=0,
            )
            rows = dot(table, rows).astype(BF).reshape(NZ, 16, 3 * NARROW)
            zs_r[half, pl.ds(to * NZ, NZ)] = rows

            for near in (0, 1, 7, 2, 6, 3, 5, 4):
                to_z = (z + near) % NZ

                def give():
                    send(
                        zs_r.at[half, to * NZ + to_z], zr_r.at[half, z * SLOTS + y], r_send,
                        zr_sem.at[half], at(to // 2, to_z, to % 2),
                    )

                if near == 0:

                    @pl.when(step > 0)
                    def _():
                        give()
                else:
                    give()

        zr_r[half, pl.ds(z * SLOTS + y, 1)] = zs_r[half, pl.ds(e * NZ + z, 1)]

    def gram_in(k):
        wait_recv(x_in.at[k, pl.ds(0, 7)], in_sem.at[k])
        add_gram(x_in, k)

    def primary_gram(k):
        @pl.when(c == 0)
        def _():
            gram_in(k)

    def put_owned():
        t0, t1 = iota((192, 192), 0), iota((192, 192), 1)
        g0 = jnp.where((t1 % 96) >= 64, 2, jnp.where((t1 % 96) >= 32, 1, 0))
        c0 = jnp.where(t1 >= 96, 1, 0)
        place = ((t1 >> 2) & 7) * 24 + c0 * 12 + g0 * 4 + (t1 & 3)
        kept = (m_owns[0:1, 0:1] > 0.5) | (c == 1)
        table = onehot((t0 == place) & kept)
        for k in range(CHUNKS):
            for b in range(4):
                rows = x_d[k, 2 * b : 2 * b + 2].reshape(192, WIDE)
                owned_ref[192 * b : 192 * (b + 1), k * WIDE : (k + 1) * WIDE] = dot(
                    table, rows
                ).astype(BF)
        store_owned.start()

    def unpack(half):
        @pl.when(c == 0)
        def _():
            wait_recv(zr_r.at[half, pl.ds(0, 31)], zr_sem.at[half])

        @pl.when(c == 1)
        def _():
            wait_recv(zr_r.at[half, pl.ds(0, 32)], zr_sem.at[half])

        for q in range(4):
            rows = zr_r[half].reshape(512, 3 * NARROW)
            rows = dot(m_back[128 * q : 128 * (q + 1)], rows) * SCALE
            for g in range(3):
                for rr in range(4):
                    first = 512 * half + NARROW * q
                    update_ref[4 * g + rr, :, first : first + NARROW] = rows[
                        32 * rr : 32 * rr + MROW, NARROW * g : NARROW * (g + 1)
                    ]
        for k in (2 * half, 2 * half + 1):
            store(1, k).start()

    pack(0)
    pl.semaphore_wait(barrier, 16)
    for step in range(1, NZ):
        pl.semaphore_signal(all_in, 1, device_id=at(y, (z + step) % NZ, c), device_id_type=MESH)
    send_first(0)
    pack(1)
    send_first(1)
    send_combined(0)
    pack(2)
    send_first(2)
    pack_own(0)
    load_momentum.wait()
    for k in range(CHUNKS):
        if k + 1 < CHUNKS:
            send_combined(k + 1)
        if k + 3 < CHUNKS:
            pack(k + 3)
            send_first(k + 3)
        if k + 1 < CHUNKS:
            pack_own(k + 1)
        gradient(k)
        forward_z(k)
        if k >= 1:
            relay_p(k - 1)
        if k >= 2:
            primary_gram(k - 2)
    forward_over_z(0)
    forward_over_z(1)
    relay_p(CHUNKS - 1)
    forward_over_z(2)
    forward_over_z(3)
    primary_gram(CHUNKS - 2)
    primary_gram(CHUNKS - 1)
    pl.semaphore_wait(all_in, NZ - 1)

    @pl.when(c == 0)
    def _():
        def between():
            relay_o(0)
            relay_o(1)

        finish(x_in, x_d, send_back, between)
        relay_o(2)
        relay_o(3)

    @pl.when(c == 1)
    def _():
        for k in range(CHUNKS):
            relay_o(k)
        for k in range(CHUNKS):
            gram_in(k)
        finish(x_in, x_d, lambda k: None, lambda: None)

    put_owned()
    for half in range(2):
        unpack(half)
    for k in range(CHUNKS):
        store(0, k).wait()
        store(1, k).wait()
    store_owned.wait()

    wait_send(s_far, x_send.at[0])
    wait_send(s_direct, x_send.at[1])
    wait_send(s_comb, x_send.at[2])
    for i, ref in enumerate((zs_f, zs_o)):
        wait_send(ref.at[:, pl.ds(0, 7)], z_send.at[i])
    wait_send(ys_p.at[:, pl.ds(0, 3)], y_send.at[0])
    wait_send(ys_o.at[:, pl.ds(0, 3)], y_send.at[2])

    @pl.when(c == 1)
    def _():
        wait_send(ys_p.at[:, 0], y_send.at[1])

    @pl.when(c == 0)
    def _():
        wait_send(ys_o.at[:, 0], y_send.at[3])
        wait_send(zs_r.at[:, pl.ds(0, 63)], r_send)


def scratch():
    def vmem(*shape, dtype=BF):
        return pltpu.VMEM(shape, dtype)

    dma = pltpu.SemaphoreType.DMA
    x_half = (2, CHUNKS, 3, 112, HALF)
    z_all = (CHUNKS, NZ, 3, 16, WIDE)
    plane = (CHUNKS, 8, 3, 32, WIDE)
    quarter = (CHUNKS, SLOTS, 3, 32, WIDE)
    return [
        vmem(12, MROW, D, dtype=F32),
        vmem(12, MROW, D, dtype=F32),
        vmem(F, D),
        vmem(CHUNKS, 12, 112, WIDE, dtype=F32),
        vmem(12, MROW, D, dtype=F32),
        *[vmem(*x_half) for _ in range(6)],
        vmem(*x_half, dtype=F32),
        vmem(CHUNKS, 3, 112, WIDE, dtype=F32),
        vmem(3, 128, WIDE, dtype=F32),
        *[vmem(*z_all) for _ in range(4)],
        vmem(2, 64, 16, 3 * NARROW),
        vmem(2, 32, 16, 3 * NARROW),
        vmem(*quarter),
        vmem(*plane),
        vmem(*plane),
        vmem(*quarter),
        vmem(*plane),
        vmem(*plane),
        vmem(F, F, dtype=F32),
        vmem(F, F),
        vmem(F, F),
        vmem(128, 128),
        vmem(128, 128),
        vmem(512, 512),
        vmem(8, 128, dtype=F32),
        dma((CHUNKS + 1,)),
        dma((3, CHUNKS)),
        dma((3,)),
        dma((2, CHUNKS)),
        dma((2, CHUNKS)),
        dma((2, CHUNKS)),
        dma((2,)),
        dma((CHUNKS,)),
        dma((CHUNKS,)),
        dma(()),
        dma((2,)),
        dma((4,)),
        dma((CHUNKS,)),
        pltpu.SemaphoreType.REGULAR,
    ]


def hand_over(*refs):
    srcs, dsts, held = refs[:3], refs[3:6], refs[6:9]
    in_sem, out_sem = refs[9:]

    def move(i, piece, src, dst, sem):
        rows = src.shape[0] // PIECES
        part = pl.ds(piece * rows, rows)
        return pltpu.make_async_copy(src.at[part], dst.at[part], sem.at[i, piece])

    each = [(i, piece) for i in range(3) for piece in range(PIECES)]
    for i, piece in each:
        move(i, piece, srcs[i], held[i], in_sem).start()
    for i, piece in each:
        move(i, piece, srcs[i], held[i], in_sem).wait()
        move(i, piece, held[i], dsts[i], out_sem).start()
    for i, piece in each:
        move(i, piece, held[i], dsts[i], out_sem).wait()


def local(partial_grads, momentum, owners):
    grads = jnp.transpose(partial_grads[0], (1, 0, 2))
    held = jnp.transpose(momentum, (1, 0, 2))
    owners = owners.reshape(1, 112)
    vmem = pl.BlockSpec(memory_space=pltpu.VMEM)
    anywhere = pl.BlockSpec(memory_space=pl.ANY)
    outs = (
        jax.ShapeDtypeStruct((12, MROW, D), F32),
        jax.ShapeDtypeStruct((12, MROW, D), F32),
        jax.ShapeDtypeStruct((F, D), BF),
    )
    results = pl.pallas_call(
        kernel,
        out_shape=outs,
        in_specs=[anywhere, anywhere, vmem],
        out_specs=(anywhere,) * 3,
        scratch_shapes=scratch(),
        compiler_params=pltpu.CompilerParams(
            collective_id=0, has_side_effects=True, vmem_limit_bytes=60 << 20
        ),
    )(grads, held, owners)
    new_momentum, update, owned = pl.pallas_call(
        hand_over,
        out_shape=outs,
        in_specs=[anywhere] * 3,
        out_specs=(anywhere,) * 3,
        scratch_shapes=[pltpu.VMEM(out.shape, out.dtype) for out in outs]
        + [pltpu.SemaphoreType.DMA((3, PIECES))] * 2,
        compiler_params=pltpu.CompilerParams(vmem_limit_bytes=60 << 20),
    )(*results)
    return (
        jnp.transpose(new_momentum, (1, 0, 2)),
        jnp.transpose(update, (1, 0, 2)),
        owned[None, None],
    )


def solution(mesh):
    return jax.shard_map(
        local,
        mesh=mesh,
        in_specs=(P("dp", None, "shard", None), P("dp", "shard", None), P()),
        out_specs=(P("dp", "shard", None), P("dp", "shard", None), P("dp", "shard", None, None)),
        check_vma=False,
    )
```

```python
import functools
import math

import jax
import jax.numpy as jnp
from jax import lax
from jax.experimental import pallas as pl
from jax.experimental.pallas import tpu as pltpu
from jax.sharding import PartitionSpec as P


MESH = pl.DeviceIdType.MESH
BF = jnp.bfloat16
F32 = jnp.float32
I32 = jnp.int32

D, F = 1024, 768
NX, NY, NZ = 4, 4, 8
MROW = 28
CHUNKS, WIDE = 4, 256
PARTS, HALF, NARROW = 6, 256, 128
CHIPS = 32
SLOTS = 4
PIECES = 4
SCALE = 0.2 * math.sqrt(max(F, D))

momentum_decay = 0.95
epsilon_norm = 1e-07
coeff_first = 3.4445
coeff_second = -4.775
coeff_third = 2.0315


def iota(shape, axis):
    return lax.broadcasted_iota(I32, shape, axis)


def onehot(cond):
    return jnp.where(cond, 1.0, 0.0).astype(BF)


def dot(a, b):
    return jnp.dot(a, b, preferred_element_type=F32)


def dot_t(a, b):
    return lax.dot_general(a, b, (((1,), (1,)), ((), ())), preferred_element_type=F32)


def routes(owner, chip_here):
    r0, r1 = iota((128, 128), 0), iota((128, 128), 1)
    owner = jnp.broadcast_to(owner[0:1], (128, 128))
    valid = r1 < MROW
    chip = jnp.where(valid, ((owner >> 1) & 7) * SLOTS + (owner >> 4), -1).astype(F32)
    core = jnp.where(valid, owner & 1, -1)
    first, second = core == 0, core == 1
    diag, before = r0 == r1, r0 < r1
    r0f = r0.astype(F32)

    def over_rows(cond, value=1.0):
        return jnp.sum(jnp.where(cond, value, 0.0), axis=0, keepdims=True)

    def over_lanes(cond, value=1.0):
        return jnp.sum(jnp.where(cond, value, 0.0), axis=1, keepdims=True)

    second_col = over_lanes(diag & second)
    nth = over_rows(before & (second_col > 0.5))
    taken = over_lanes(first & (chip == r0f))
    free = jnp.where((r0[:, 0:1] < NZ * SLOTS) & (taken < 0.5), 1.0, 0.0)
    free_row = over_rows(diag & (free > 0.5))
    free_before = over_lanes((r1 < r0) & (free_row > 0.5))
    away = over_rows((free > 0.5) & (free_before == nth), r0f)
    first, second, valid, chip = first[0:1], second[0:1], valid[0:1], chip[0:1]
    code = jnp.where(first, chip, jnp.where(second, away, -1.0))
    code_over = jnp.where(second, chip, -1.0)
    owns = jnp.sum(
        jnp.where(first & (chip == chip_here.astype(F32)), 1.0, 0.0), axis=1, keepdims=True
    )

    def tiled(row):
        row = jnp.where(valid, row, -1.0)
        wide = jnp.broadcast_to(row, (8, 128))
        out = wide
        for turn in (1, 2, 3):
            lane = iota((8, 128), 1)
            out = jnp.where((lane >> 5) == turn, pltpu.roll(wide, 32 * turn, 1), out)
        return out[0:1]

    f0, f1 = iota((512, 128), 0), iota((512, 128), 1)
    same_row = ((f0 >> 2) & 3) == (f1 >> 5)
    chip_at = (f0 >> 4).astype(F32)

    def outward(row):
        meant = same_row & (tiled(row) == chip_at)
        return [onehot(meant & ((f0 & 3) == q)) for q in range(4)]

    forward, forward_over = outward(code), outward(code_over)
    code_col = jnp.sum(
        jnp.where(r1 == (r0 & 31), jnp.broadcast_to(code, (128, 128)), 0.0), axis=1, keepdims=True
    )
    code_col = jnp.where((r0[:, 0:1] & 31) < MROW, code_col, -1.0)
    b0, b1 = iota((128, 512), 0), iota((128, 512), 1)
    whose = ((b0 >> 5) == ((b1 >> 2) & 3)) & (code_col == (b1 >> 4).astype(F32))
    back = [onehot(whose & ((b1 & 3) == q)) for q in range(4)]
    return forward, forward_over, back, owns


def kernel(
    grads_hbm,
    momentum_hbm,
    owners_ref,
    newm_hbm,
    update_hbm,
    owned_hbm,
    newm_ref,
    update_ref,
    owned_ref,
    grads,
    momentum,
    s_direct,
    s_far,
    s_comb,
    r_direct,
    r_far,
    r_comb,
    part,
    own,
    nest,
    zs_f,
    zs_o,
    raw,
    zs_r,
    zr_r,
    x_in,
    x_d,
    x_a,
    x_b,
    gram_f,
    gram_b,
    poly_b,
    m_forward,
    m_over,
    m_back,
    m_owns,
    load_sem,
    store_sem,
    x_send,
    direct_sem,
    far_sem,
    comb_sem,
    z_send,
    r_send,
    zr_sem,
    in_sem,
    all_in,
):
    x = lax.axis_index("dp")
    here = lax.axis_index("shard")
    y, z, c = here // 16, (here // 2) % NZ, here % 2
    e = 2 * y + c
    right, left, far = (x + 1) % NX, (x + 3) % NX, (x + 2) % NX

    def at(y_, z_, c_):
        return (x, (y_ * NZ + z_) * 2 + c_)

    def send(src, dst, send_sem, recv_sem, device):
        pltpu.make_async_remote_copy(
            src_ref=src, dst_ref=dst, send_sem=send_sem, recv_sem=recv_sem,
            device_id=device, device_id_type=MESH,
        ).start()

    def wait_recv(ref, sem):
        pltpu.make_async_remote_copy(
            src_ref=ref, dst_ref=ref, send_sem=sem, recv_sem=sem,
            device_id=(x, here), device_id_type=MESH,
        ).wait_recv()

    def wait_send(ref, sem):
        pltpu.make_async_remote_copy(
            src_ref=ref, dst_ref=ref, send_sem=sem, recv_sem=sem,
            device_id=(x, here), device_id_type=MESH,
        ).wait_send()

    def load(k):
        return pltpu.make_async_copy(
            grads_hbm.at[pl.ds(4 * (k % 3), 4), :, pl.ds(512 * (k // 3), 512)],
            grads.at[k],
            load_sem.at[k],
        )

    load_momentum = pltpu.make_async_copy(momentum_hbm, momentum, load_sem.at[PARTS])
    for k in range(PARTS):
        load(k).start()
    load_momentum.start()

    def store(i, half):
        src, dst = ((newm_ref, newm_hbm), (update_ref, update_hbm))[i]
        cols = pl.ds(512 * half, 512)
        return pltpu.make_async_copy(src.at[:, :, cols], dst.at[:, :, cols], store_sem.at[i, half])

    store_owned = pltpu.make_async_copy(owned_ref, owned_hbm, store_sem.at[2, 0])

    barrier = pltpu.get_barrier_semaphore()
    for device in ((right, here), (left, here)):
        pl.semaphore_signal(barrier, 1, device_id=device, device_id_type=MESH)
    for step in range(1, NZ):
        pl.semaphore_signal(barrier, 1, device_id=at(y, (z + step) % NZ, c), device_id_type=MESH)
    for step in range(1, 8):
        other = (e + step) % 8
        pl.semaphore_signal(
            barrier, 1, device_id=at(other // 2, z, other % 2), device_id_type=MESH
        )

    def make_tables():
        owner = jnp.concatenate([owners_ref[...], jnp.zeros((1, 16), I32)], axis=1)
        owner = pltpu.roll(jnp.broadcast_to(owner, (8, 128)), (128 - MROW * x) % 128, 1)
        forward, forward_over, back, owns = routes(owner, z * SLOTS + y)
        for q in range(4):
            m_forward[:, 128 * q : 128 * (q + 1)] = forward[q]
            m_over[:, 128 * q : 128 * (q + 1)] = forward_over[q]
            m_back[128 * q : 128 * (q + 1)] = back[q]
        m_owns[...] = jnp.broadcast_to(owns, (8, 128))
        nest[...] = jnp.zeros_like(nest)

    p0, p1 = iota((112, 128), 0), iota((112, 128), 1)
    quarter = (
        jnp.where(p0 >= 28, 1, 0) + jnp.where(p0 >= 56, 1, 0) + jnp.where(p0 >= 84, 1, 0)
    )

    def packing(parity):
        return onehot(p1 == p0 + 4 * quarter + 4 * parity)

    def window(k, to, table):
        start = pl.multiple_of(((MROW * to) // 8) * 8, 8)
        rows = grads[k, :, pl.ds(start, 32), :].astype(BF).reshape(128, 2 * HALF)
        return dot(table, rows)

    def pack(k):
        load(k).wait()
        odd = packing((x + 1) % 2)
        even = packing(x % 2)
        v = window(k, far, even).astype(BF)
        s_far[0, k] = v[:, :HALF]
        s_far[1, k] = v[:, HALF:]
        v = window(k, right, odd)
        part[0, k] = v[:, :HALF]
        s_direct[0, k] = v[:, HALF:].astype(BF)
        v = window(k, left, odd)
        part[1, k] = v[:, HALF:]
        s_direct[1, k] = v[:, :HALF].astype(BF)

    def pack_own(k):
        own[k] = window(k, x, packing(x % 2))

    towards = ((right, here), (left, here))

    def send_first(k):
        for way in range(2):
            send(s_far.at[way, k], r_far.at[way, k], x_send.at[0], far_sem.at[way, k], towards[way])
        for way in range(2):
            send(
                s_direct.at[way, k], r_direct.at[way, k], x_send.at[1], direct_sem.at[way, k],
                towards[way],
            )

    def send_combined(k):
        for way in range(2):
            wait_recv(r_far.at[way, k], far_sem.at[way, k])
            s_comb[way, k] = (part[way, k] + r_far[way, k].astype(F32)).astype(BF)
            send(
                s_comb.at[way, k], r_comb.at[way, k], x_send.at[2], comb_sem.at[way, k],
                towards[way],
            )

    def gradient(k):
        for way in range(2):
            wait_recv(r_direct.at[way, k], direct_sem.at[way, k])
            wait_recv(r_comb.at[way, k], comb_sem.at[way, k])
        low = own[k, :, :HALF] + r_direct[1, k].astype(F32) + r_comb[0, k].astype(F32)
        high = own[k, :, HALF:] + r_direct[0, k].astype(F32) + r_comb[1, k].astype(F32)
        own[k, :, :HALF] = low
        own[k, :, HALF:] = high
        g, half = k % 3, k // 3
        cols = slice(512 * half, 512 * (half + 1))
        for rr in range(4):
            total = own[k, MROW * rr : MROW * (rr + 1), :]
            moved = momentum_decay * momentum[4 * g + rr, :, cols] + total
            newm_ref[4 * g + rr, :, cols] = moved
            nest[32 * rr : 32 * rr + MROW, :] = total + momentum_decay * moved
        if g == 2:
            store(0, half).start()

    def send_out(k, zs, core, sem):
        @pl.loop(0, CHIPS)
        def _(i):
            j = i // 4
            to_z = (z + 4 + (1 - 2 * (j % 2)) * ((j + 1) // 2)) % NZ
            to_y = (y + i) % NY

            @pl.when(jnp.logical_or(i != 28, c != core))
            def _():
                send(
                    zs.at[k, to_z * SLOTS + to_y], raw.at[k, here], sem, in_sem.at[k],
                    at(to_y, to_z, core),
                )

        @pl.when(c == core)
        def _():
            raw[k, pl.ds(here, 1)] = zs[k, pl.ds(z * SLOTS + y, 1)]

    def rows_out(k):
        rows = nest[...].astype(BF)
        rows = jnp.concatenate([rows[:, NARROW * q : NARROW * (q + 1)] for q in range(4)], axis=0)
        zs_f[k] = dot(m_forward[...], rows).astype(BF).reshape(CHIPS, 16, NARROW)
        send_out(k, zs_f, 0, z_send.at[0])
        zs_o[k] = dot(m_over[...], rows).astype(BF).reshape(CHIPS, 16, NARROW)

    def rows_out_over(k):
        send_out(k, zs_o, 1, z_send.at[1])

    i0, i1 = iota((128, 128), 0), iota((128, 128), 1)
    to_columns = lambda: onehot(i1 == ((i0 & 31) << 2) + (i0 >> 5))
    from_columns = lambda: onehot(i0 == ((i1 & 31) << 2) + (i1 >> 5))

    def rows_in(k):
        wait_recv(raw.at[k, pl.ds(0, 63)], in_sem.at[k])
        g, half = k % 3, k // 3
        rows = jnp.concatenate(
            [raw[k, 8 * i : 8 * (i + 1)].reshape(128, NARROW) for i in range(8)], axis=1
        )
        rows = dot(to_columns(), rows).astype(BF)
        for q in range(4):
            for i in range(8):
                first = 256 * g + 32 * i
                x_in[
                    2 * half + q // 2, first : first + 32,
                    NARROW * (q % 2) : NARROW * (q % 2 + 1),
                ] = rows[32 * q : 32 * (q + 1), NARROW * i : NARROW * (i + 1)]
        if g == 2:
            add_gram(x_in, 2 * half)
            add_gram(x_in, 2 * half + 1)

    def matrix(ref, k):
        return ref[k]

    blocks = [(i, j) for i in range(3) for j in range(i, 3)]

    def block(ref, i, j):
        return ref.at[256 * i : 256 * (i + 1), 256 * j : 256 * (j + 1)]

    def add_gram(src, k):
        rows = matrix(src, k)
        for i, j in blocks:
            new = dot_t(rows[256 * i : 256 * (i + 1)], rows[256 * j : 256 * (j + 1)])
            into = block(gram_f, i, j)
            into[...] = new if k == 0 else into[...] + new

    def put_gram(i, j, value):
        value = value.astype(BF)
        block(gram_b, i, j)[...] = value
        if i != j:
            block(gram_b, j, i)[...] = value.T

    def whole_gram(src):
        for i, j in blocks:
            total = 0.0
            for k in range(CHUNKS):
                rows = matrix(src, k)
                total = total + dot_t(
                    rows[256 * i : 256 * (i + 1)], rows[256 * j : 256 * (j + 1)]
                )
            put_gram(i, j, total)

    def poly():
        for i, j in blocks:
            square = dot(
                gram_b[256 * i : 256 * (i + 1), :], gram_b[:, 256 * j : 256 * (j + 1)]
            )
            value = coeff_second * block(gram_b, i, j)[...].astype(F32) + coeff_third * square
            value = value.astype(BF)
            block(poly_b, i, j)[...] = value
            if i != j:
                block(poly_b, j, i)[...] = value.T

    def advance(src, dst, k):
        rows = matrix(src, k)
        out = coeff_first * rows.astype(F32) + dot(poly_b[...], rows)
        dst[k] = out.astype(BF)

    def finish(src, dst, done, between):
        d0, d1 = iota((256, 256), 0), iota((256, 256), 1)
        squares = 0.0
        for i in range(3):
            squares = squares + jnp.sum(jnp.where(d0 == d1, block(gram_f, i, i)[...], 0.0))
        inverse = 1.0 / (jnp.sqrt(squares) + epsilon_norm)
        for i, j in blocks:
            put_gram(i, j, block(gram_f, i, j)[...] * (inverse * inverse))
        for k in range(CHUNKS):
            x_a[k] = (src[k].astype(F32) * inverse).astype(BF)
        poly()
        for k in range(CHUNKS):
            advance(x_a, x_b, k)
        between()
        whole_gram(x_b)
        poly()
        for k in range(CHUNKS):
            advance(x_b, dst, k)
            done(k)

    def send_back(k):
        if k % 2 == 0:
            return
        half = k // 2
        table = from_columns()

        @pl.loop(0, 8)
        def _(step):
            group = (here // 8 + step) % 8
            rows = jnp.concatenate(
                [
                    jnp.concatenate(
                        [
                            x_d[
                                k - 1 + q // 2,
                                pl.ds(pl.multiple_of(256 * g + 32 * group, 32), 32),
                                NARROW * (q % 2) : NARROW * (q % 2 + 1),
                            ]
                            for g in range(3)
                        ],
                        axis=1,
                    )
                    for q in range(4)
                ],
                axis=0,
            )
            rows = dot(table, rows).astype(BF).reshape(8, 16, 3 * NARROW)
            zs_r[half, pl.ds(group * 8, 8)] = rows

            @pl.loop(0, 8)
            def _(i):
                to = group * 8 + i

                @pl.when(to != here)
                def _():
                    send(
                        zs_r.at[half, to], zr_r.at[half, z * SLOTS + y], r_send, zr_sem.at[half],
                        (x, to),
                    )

        zr_r[half, pl.ds(z * SLOTS + y, 1)] = zs_r[half, pl.ds(here, 1)]

    def primary_in(k):
        @pl.when(c == 0)
        def _():
            rows_in(k)

    def put_owned():
        t0, t1 = iota((192, 192), 0), iota((192, 192), 1)
        place = ((t1 & 63) >> 2) * 12 + (t1 >> 6) * 4 + (t1 & 3)
        kept = (m_owns[0:1, 0:1] > 0.5) | (c == 1)
        table = onehot((t0 == place) & kept)
        for k in range(CHUNKS):
            for b in range(4):
                rows = jnp.concatenate(
                    [x_d[k, 256 * g + 64 * b : 256 * g + 64 * (b + 1)] for g in range(3)], axis=0
                )
                owned_ref[192 * b : 192 * (b + 1), k * WIDE : (k + 1) * WIDE] = dot(
                    table, rows
                ).astype(BF)
        store_owned.start()

    def unpack(half):
        @pl.when(c == 0)
        def _():
            wait_recv(zr_r.at[half, pl.ds(0, 31)], zr_sem.at[half])

        @pl.when(c == 1)
        def _():
            wait_recv(zr_r.at[half, pl.ds(0, 32)], zr_sem.at[half])

        for q in range(4):
            rows = zr_r[half].reshape(512, 3 * NARROW)
            rows = dot(m_back[128 * q : 128 * (q + 1)], rows) * SCALE
            for g in range(3):
                for rr in range(4):
                    first = 512 * half + NARROW * q
                    update_ref[4 * g + rr, :, first : first + NARROW] = rows[
                        32 * rr : 32 * rr + MROW, NARROW * g : NARROW * (g + 1)
                    ]
        store(1, half).start()

    pack(0)
    pl.semaphore_wait(barrier, 16)
    for step in range(1, NZ):
        pl.semaphore_signal(all_in, 1, device_id=at(y, (z + step) % NZ, c), device_id_type=MESH)
    send_first(0)
    pack(1)
    send_first(1)
    send_combined(0)
    pack(2)
    send_first(2)
    pack_own(0)
    make_tables()
    load_momentum.wait()
    for k in range(PARTS):
        if k + 1 < PARTS:
            send_combined(k + 1)
        if k + 3 < PARTS:
            pack(k + 3)
            send_first(k + 3)
        if k + 1 < PARTS:
            pack_own(k + 1)
        gradient(k)
        if k == 0:
            pl.semaphore_wait(all_in, NZ - 1)
        rows_out(k)
        if k >= 2:
            primary_in(k - 2)
    rows_out_over(0)
    rows_out_over(1)
    primary_in(PARTS - 2)
    rows_out_over(2)
    rows_out_over(3)
    rows_out_over(4)
    rows_out_over(5)

    @pl.when(c == 0)
    def _():
        rows_in(PARTS - 1)
        finish(x_in, x_d, send_back, lambda: None)

    @pl.when(c == 1)
    def _():
        for k in range(PARTS):
            rows_in(k)
        finish(x_in, x_d, lambda k: None, lambda: None)

    put_owned()
    for half in range(2):
        unpack(half)
    for half in range(2):
        store(0, half).wait()
        store(1, half).wait()
    store_owned.wait()

    wait_send(s_far, x_send.at[0])
    wait_send(s_direct, x_send.at[1])
    wait_send(s_comb, x_send.at[2])

    @pl.when(c == 0)
    def _():
        wait_send(zs_f.at[:, pl.ds(0, CHIPS - 1)], z_send.at[0])
        wait_send(zs_o, z_send.at[1])
        wait_send(zs_r.at[:, pl.ds(0, 63)], r_send)

    @pl.when(c == 1)
    def _():
        wait_send(zs_f, z_send.at[0])
        wait_send(zs_o.at[:, pl.ds(0, CHIPS - 1)], z_send.at[1])


def scratch():
    def vmem(*shape, dtype=BF):
        return pltpu.VMEM(shape, dtype)

    dma = pltpu.SemaphoreType.DMA
    x_half = (2, PARTS, 112, HALF)
    whole = (CHUNKS, F, WIDE)
    return [
        vmem(12, MROW, D, dtype=F32),
        vmem(12, MROW, D, dtype=F32),
        vmem(F, D),
        vmem(PARTS, 4, 112, 512, dtype=F32),
        vmem(12, MROW, D, dtype=F32),
        *[vmem(*x_half) for _ in range(6)],
        vmem(*x_half, dtype=F32),
        vmem(PARTS, 112, 512, dtype=F32),
        vmem(128, 512, dtype=F32),
        vmem(PARTS, CHIPS, 16, NARROW),
        vmem(PARTS, CHIPS, 16, NARROW),
        vmem(PARTS, 64, 16, NARROW),
        vmem(2, 64, 16, 3 * NARROW),
        vmem(2, CHIPS, 16, 3 * NARROW),
        vmem(*whole),
        vmem(*whole),
        vmem(*whole),
        vmem(*whole),
        vmem(F, F, dtype=F32),
        vmem(F, F),
        vmem(F, F),
        vmem(512, 512),
        vmem(512, 512),
        vmem(512, 512),
        vmem(8, 128, dtype=F32),
        dma((PARTS + 1,)),
        dma((3, 2)),
        dma((3,)),
        dma((2, PARTS)),
        dma((2, PARTS)),
        dma((2, PARTS)),
        dma((2,)),
        dma(()),
        dma((2,)),
        dma((PARTS,)),
        pltpu.SemaphoreType.REGULAR,
    ]


def hand_over(*refs):
    srcs, dsts, held = refs[:3], refs[3:6], refs[6:9]
    in_sem, out_sem = refs[9:]

    def move(i, piece, src, dst, sem):
        rows = src.shape[0] // PIECES
        part = pl.ds(piece * rows, rows)
        return pltpu.make_async_copy(src.at[part], dst.at[part], sem.at[i, piece])

    each = [(i, piece) for i in range(3) for piece in range(PIECES)]
    for i, piece in each:
        move(i, piece, srcs[i], held[i], in_sem).start()
    for i, piece in each:
        move(i, piece, srcs[i], held[i], in_sem).wait()
        move(i, piece, held[i], dsts[i], out_sem).start()
    for i, piece in each:
        move(i, piece, held[i], dsts[i], out_sem).wait()


def local(partial_grads, momentum, owners):
    grads = jnp.transpose(partial_grads[0], (1, 0, 2))
    held = jnp.transpose(momentum, (1, 0, 2))
    owners = owners.reshape(1, 112)
    vmem = pl.BlockSpec(memory_space=pltpu.VMEM)
    anywhere = pl.BlockSpec(memory_space=pl.ANY)
    outs = (
        jax.ShapeDtypeStruct((12, MROW, D), F32),
        jax.ShapeDtypeStruct((12, MROW, D), F32),
        jax.ShapeDtypeStruct((F, D), BF),
    )
    results = pl.pallas_call(
        kernel,
        out_shape=outs,
        in_specs=[anywhere, anywhere, vmem],
        out_specs=(anywhere,) * 3,
        scratch_shapes=scratch(),
        compiler_params=pltpu.CompilerParams(
            collective_id=0, has_side_effects=True, vmem_limit_bytes=60 << 20
        ),
    )(grads, held, owners)
    new_momentum, update, owned = pl.pallas_call(
        hand_over,
        out_shape=outs,
        in_specs=[anywhere] * 3,
        out_specs=(anywhere,) * 3,
        scratch_shapes=[pltpu.VMEM(out.shape, out.dtype) for out in outs]
        + [pltpu.SemaphoreType.DMA((3, PIECES))] * 2,
        compiler_params=pltpu.CompilerParams(vmem_limit_bytes=60 << 20),
    )(*results)
    return (
        jnp.transpose(new_momentum, (1, 0, 2)),
        jnp.transpose(update, (1, 0, 2)),
        owned[None, None],
    )


def solution(mesh):
    return jax.shard_map(
        local,
        mesh=mesh,
        in_specs=(P("dp", None, "shard", None), P("dp", "shard", None), P()),
        out_specs=(P("dp", "shard", None), P("dp", "shard", None), P("dp", "shard", None, None)),
        check_vma=False,
    )
```

```python
import functools
import math

import jax
import jax.numpy as jnp
from jax import lax
from jax.experimental import pallas as pl
from jax.experimental.pallas import tpu as pltpu
from jax.sharding import PartitionSpec as P


MESH = pl.DeviceIdType.MESH
BF = jnp.bfloat16
F32 = jnp.float32
I32 = jnp.int32

D, F = 1024, 768
NX, NY, NZ = 4, 4, 8
MROW = 28
CHUNKS, WIDE = 4, 256
PARTS, HALF, NARROW = 6, 256, 128
CHIPS = 32
SLOTS = 4
PIECES = 4
LIMIT = 48
SCALE = 0.2 * math.sqrt(max(F, D))

momentum_decay = 0.95
epsilon_norm = 1e-07
coeff_first = 3.4445
coeff_second = -4.775
coeff_third = 2.0315


def iota(shape, axis):
    return lax.broadcasted_iota(I32, shape, axis)


def onehot(cond):
    return jnp.where(cond, 1.0, 0.0).astype(BF)


def dot(a, b):
    return jnp.dot(a, b, preferred_element_type=F32)


def dot_t(a, b):
    return lax.dot_general(a, b, (((1,), (1,)), ((), ())), preferred_element_type=F32)


def routes(owner, chip_here):
    r0, r1 = iota((128, 128), 0), iota((128, 128), 1)
    owner = jnp.broadcast_to(owner[0:1], (128, 128))
    valid = r1 < MROW
    chip = jnp.where(valid, ((owner >> 1) & 7) * SLOTS + (owner >> 4), -1).astype(F32)
    core = jnp.where(valid, owner & 1, -1)
    first, second = core == 0, core == 1
    diag, before = r0 == r1, r0 < r1
    r0f = r0.astype(F32)

    def over_rows(cond, value=1.0):
        return jnp.sum(jnp.where(cond, value, 0.0), axis=0, keepdims=True)

    def over_lanes(cond, value=1.0):
        return jnp.sum(jnp.where(cond, value, 0.0), axis=1, keepdims=True)

    second_col = over_lanes(diag & second)
    nth = over_rows(before & (second_col > 0.5))
    taken = over_lanes(first & (chip == r0f))
    free = jnp.where((r0[:, 0:1] < NZ * SLOTS) & (taken < 0.5), 1.0, 0.0)
    free_row = over_rows(diag & (free > 0.5))
    free_before = over_lanes((r1 < r0) & (free_row > 0.5))
    away = over_rows((free > 0.5) & (free_before == nth), r0f)
    first, second, valid, chip = first[0:1], second[0:1], valid[0:1], chip[0:1]
    code = jnp.where(first, chip, jnp.where(second, away, -1.0))
    code_over = jnp.where(second, chip, -1.0)
    owns = jnp.sum(
        jnp.where(first & (chip == chip_here.astype(F32)), 1.0, 0.0), axis=1, keepdims=True
    )

    def tiled(row):
        row = jnp.where(valid, row, -1.0)
        wide = jnp.broadcast_to(row, (8, 128))
        out = wide
        for turn in (1, 2, 3):
            lane = iota((8, 128), 1)
            out = jnp.where((lane >> 5) == turn, pltpu.roll(wide, 32 * turn, 1), out)
        return out[0:1]

    f0, f1 = iota((512, 128), 0), iota((512, 128), 1)
    same_row = ((f0 >> 2) & 3) == (f1 >> 5)
    chip_at = (f0 >> 4).astype(F32)

    def outward(row):
        meant = same_row & (tiled(row) == chip_at)
        return [onehot(meant & ((f0 & 3) == q)) for q in range(4)]

    forward, forward_over = outward(code), outward(code_over)
    code_col = jnp.sum(
        jnp.where(r1 == (r0 & 31), jnp.broadcast_to(code, (128, 128)), 0.0), axis=1, keepdims=True
    )
    code_col = jnp.where((r0[:, 0:1] & 31) < MROW, code_col, -1.0)
    b0, b1 = iota((128, 512), 0), iota((128, 512), 1)
    whose = ((b0 >> 5) == ((b1 >> 2) & 3)) & (code_col == (b1 >> 4).astype(F32))
    back = [onehot(whose & ((b1 & 3) == q)) for q in range(4)]
    return forward, forward_over, back, owns


def kernel(
    grads_hbm,
    momentum_hbm,
    owners_ref,
    newm_ref,
    update_ref,
    owned_ref,
    grads,
    momentum,
    s_direct,
    s_far,
    s_comb,
    r_direct,
    r_far,
    r_comb,
    part,
    own,
    nest,
    zs_f,
    zs_o,
    raw,
    zs_r,
    zr_r,
    x_in,
    x_d,
    x_b,
    gram_f,
    gram_b,
    poly_b,
    m_forward,
    m_over,
    m_back,
    m_owns,
    load_sem,
    x_send,
    direct_sem,
    far_sem,
    comb_sem,
    z_send,
    r_send,
    zr_sem,
    in_sem,
    all_in,
):
    x = lax.axis_index("dp")
    here = lax.axis_index("shard")
    y, z, c = here // 16, (here // 2) % NZ, here % 2
    e = 2 * y + c
    right, left, far = (x + 1) % NX, (x + 3) % NX, (x + 2) % NX

    def at(y_, z_, c_):
        return (x, (y_ * NZ + z_) * 2 + c_)

    def send(src, dst, send_sem, recv_sem, device):
        pltpu.make_async_remote_copy(
            src_ref=src, dst_ref=dst, send_sem=send_sem, recv_sem=recv_sem,
            device_id=device, device_id_type=MESH,
        ).start()

    def wait_recv(ref, sem):
        pltpu.make_async_remote_copy(
            src_ref=ref, dst_ref=ref, send_sem=sem, recv_sem=sem,
            device_id=(x, here), device_id_type=MESH,
        ).wait_recv()

    def wait_send(ref, sem):
        pltpu.make_async_remote_copy(
            src_ref=ref, dst_ref=ref, send_sem=sem, recv_sem=sem,
            device_id=(x, here), device_id_type=MESH,
        ).wait_send()

    def load(k):
        return pltpu.make_async_copy(
            grads_hbm.at[pl.ds(4 * (k % 3), 4), :, pl.ds(512 * (k // 3), 512)],
            grads.at[k],
            load_sem.at[k],
        )

    load_momentum = pltpu.make_async_copy(momentum_hbm, momentum, load_sem.at[PARTS])
    for k in range(PARTS):
        load(k).start()
    load_momentum.start()

    barrier = pltpu.get_barrier_semaphore()
    for device in ((right, here), (left, here)):
        pl.semaphore_signal(barrier, 1, device_id=device, device_id_type=MESH)
    for step in range(1, NZ):
        pl.semaphore_signal(barrier, 1, device_id=at(y, (z + step) % NZ, c), device_id_type=MESH)
    for step in range(1, 8):
        other = (e + step) % 8
        pl.semaphore_signal(
            barrier, 1, device_id=at(other // 2, z, other % 2), device_id_type=MESH
        )

    def make_tables():
        owner = jnp.concatenate([owners_ref[...], jnp.zeros((1, 16), I32)], axis=1)
        owner = pltpu.roll(jnp.broadcast_to(owner, (8, 128)), (128 - MROW * x) % 128, 1)
        forward, forward_over, back, owns = routes(owner, z * SLOTS + y)
        for q in range(4):
            m_forward[:, 128 * q : 128 * (q + 1)] = forward[q]
            m_over[:, 128 * q : 128 * (q + 1)] = forward_over[q]
            m_back[128 * q : 128 * (q + 1)] = back[q]
        m_owns[...] = jnp.broadcast_to(owns, (8, 128))
        nest[...] = jnp.zeros_like(nest)

    p0, p1 = iota((112, 128), 0), iota((112, 128), 1)
    quarter = (
        jnp.where(p0 >= 28, 1, 0) + jnp.where(p0 >= 56, 1, 0) + jnp.where(p0 >= 84, 1, 0)
    )

    def packing(parity):
        return onehot(p1 == p0 + 4 * quarter + 4 * parity)

    def window(k, to, table):
        start = pl.multiple_of(((MROW * to) // 8) * 8, 8)
        rows = grads[k, :, pl.ds(start, 32), :].astype(BF).reshape(128, 2 * HALF)
        return dot(table, rows)

    def pack(k):
        load(k).wait()
        odd = packing((x + 1) % 2)
        even = packing(x % 2)
        v = window(k, far, even).astype(BF)
        s_far[0, k] = v[:, :HALF]
        s_far[1, k] = v[:, HALF:]
        v = window(k, right, odd)
        part[0, k] = v[:, :HALF]
        s_direct[0, k] = v[:, HALF:].astype(BF)
        v = window(k, left, odd)
        part[1, k] = v[:, HALF:]
        s_direct[1, k] = v[:, :HALF].astype(BF)

    def pack_own(k):
        own[k] = window(k, x, packing(x % 2))

    towards = ((right, here), (left, here))

    def send_first(k):
        for way in range(2):
            send(s_far.at[way, k], r_far.at[way, k], x_send.at[0], far_sem.at[way, k], towards[way])
        for way in range(2):
            send(
                s_direct.at[way, k], r_direct.at[way, k], x_send.at[1], direct_sem.at[way, k],
                towards[way],
            )

    def send_combined(k):
        for way in range(2):
            wait_recv(r_far.at[way, k], far_sem.at[way, k])
            s_comb[way, k] = (part[way, k] + r_far[way, k].astype(F32)).astype(BF)
            send(
                s_comb.at[way, k], r_comb.at[way, k], x_send.at[2], comb_sem.at[way, k],
                towards[way],
            )

    def gradient(k):
        for way in range(2):
            wait_recv(r_direct.at[way, k], direct_sem.at[way, k])
            wait_recv(r_comb.at[way, k], comb_sem.at[way, k])
        low = own[k, :, :HALF] + r_direct[1, k].astype(F32) + r_comb[0, k].astype(F32)
        high = own[k, :, HALF:] + r_direct[0, k].astype(F32) + r_comb[1, k].astype(F32)
        own[k, :, :HALF] = low
        own[k, :, HALF:] = high
        g, half = k % 3, k // 3
        cols = slice(512 * half, 512 * (half + 1))
        for rr in range(4):
            total = own[k, MROW * rr : MROW * (rr + 1), :]
            moved = momentum_decay * momentum[4 * g + rr, :, cols] + total
            newm_ref[4 * g + rr, :, cols] = moved
            nest[32 * rr : 32 * rr + MROW, :] = total + momentum_decay * moved

    def send_out(k, zs, core, sem):
        @pl.loop(0, CHIPS)
        def _(i):
            j = i // 4
            to_z = (z + 4 + (1 - 2 * (j % 2)) * ((j + 1) // 2)) % NZ
            to_y = (y + i) % NY

            @pl.when(jnp.logical_or(i != 28, c != core))
            def _():
                send(
                    zs.at[k, to_z * SLOTS + to_y], raw.at[k, here], sem, in_sem.at[k],
                    at(to_y, to_z, core),
                )

        @pl.when(c == core)
        def _():
            raw[k, pl.ds(here, 1)] = zs[k, pl.ds(z * SLOTS + y, 1)]

    def rows_out(k):
        rows = nest[...].astype(BF)
        rows = jnp.concatenate([rows[:, NARROW * q : NARROW * (q + 1)] for q in range(4)], axis=0)
        zs_f[k] = dot(m_forward[...], rows).astype(BF).reshape(CHIPS, 16, NARROW)
        send_out(k, zs_f, 0, z_send.at[0])
        zs_o[k] = dot(m_over[...], rows).astype(BF).reshape(CHIPS, 16, NARROW)

    def rows_out_over(k):
        send_out(k, zs_o, 1, z_send.at[1])

    i0, i1 = iota((128, 128), 0), iota((128, 128), 1)
    to_columns = lambda: onehot(i1 == ((i0 & 31) << 2) + (i0 >> 5))
    from_columns = lambda: onehot(i0 == ((i1 & 31) << 2) + (i1 >> 5))

    def rows_in(k):
        wait_recv(raw.at[k, pl.ds(0, 63)], in_sem.at[k])
        g, half = k % 3, k // 3
        rows = jnp.concatenate(
            [raw[k, 8 * i : 8 * (i + 1)].reshape(128, NARROW) for i in range(8)], axis=1
        )
        rows = dot(to_columns(), rows).astype(BF)
        for q in range(4):
            for i in range(8):
                first = 256 * g + 32 * i
                x_in[
                    2 * half + q // 2, first : first + 32,
                    NARROW * (q % 2) : NARROW * (q % 2 + 1),
                ] = rows[32 * q : 32 * (q + 1), NARROW * i : NARROW * (i + 1)]
        if g == 2:
            add_gram(x_in, 2 * half)
            add_gram(x_in, 2 * half + 1)

    def matrix(ref, k):
        return ref[k]

    blocks = [(i, j) for i in range(3) for j in range(i, 3)]

    def block(ref, i, j):
        return ref.at[256 * i : 256 * (i + 1), 256 * j : 256 * (j + 1)]

    def add_gram(src, k):
        rows = matrix(src, k)
        for i, j in blocks:
            new = dot_t(rows[256 * i : 256 * (i + 1)], rows[256 * j : 256 * (j + 1)])
            into = block(gram_f, i, j)
            into[...] = new if k == 0 else into[...] + new

    def put_gram(i, j, value):
        value = value.astype(BF)
        block(gram_b, i, j)[...] = value
        if i != j:
            block(gram_b, j, i)[...] = value.T

    def whole_gram(src):
        for i, j in blocks:
            total = 0.0
            for k in range(CHUNKS):
                rows = matrix(src, k)
                total = total + dot_t(
                    rows[256 * i : 256 * (i + 1)], rows[256 * j : 256 * (j + 1)]
                )
            put_gram(i, j, total)

    def poly():
        for i, j in blocks:
            square = dot(
                gram_b[256 * i : 256 * (i + 1), :], gram_b[:, 256 * j : 256 * (j + 1)]
            )
            value = coeff_second * block(gram_b, i, j)[...].astype(F32) + coeff_third * square
            value = value.astype(BF)
            block(poly_b, i, j)[...] = value
            if i != j:
                block(poly_b, j, i)[...] = value.T

    def advance(src, dst, k, scale=None):
        rows = matrix(src, k)
        out = coeff_first * rows.astype(F32) + dot(poly_b[...], rows)
        if scale is not None:
            out = out * scale
        dst[k] = out.astype(BF)

    def finish(src, dst, done, between):
        d0, d1 = iota((256, 256), 0), iota((256, 256), 1)
        squares = 0.0
        for i in range(3):
            squares = squares + jnp.sum(jnp.where(d0 == d1, block(gram_f, i, i)[...], 0.0))
        inverse = 1.0 / (jnp.sqrt(squares) + epsilon_norm)
        for i, j in blocks:
            put_gram(i, j, block(gram_f, i, j)[...] * (inverse * inverse))
        poly()
        for k in range(CHUNKS):
            advance(src, x_b, k, inverse)
        between()
        whole_gram(x_b)
        poly()
        for k in range(CHUNKS):
            advance(x_b, dst, k)
            done(k)

    def send_back(k):
        if k % 2 == 0:
            return
        half = k // 2
        table = from_columns()

        @pl.loop(0, 8)
        def _(step):
            group = (here // 8 + step) % 8
            rows = jnp.concatenate(
                [
                    jnp.concatenate(
                        [
                            x_d[
                                k - 1 + q // 2,
                                pl.ds(pl.multiple_of(256 * g + 32 * group, 32), 32),
                                NARROW * (q % 2) : NARROW * (q % 2 + 1),
                            ]
                            for g in range(3)
                        ],
                        axis=1,
                    )
                    for q in range(4)
                ],
                axis=0,
            )
            rows = dot(table, rows).astype(BF).reshape(8, 16, 3 * NARROW)
            zs_r[half, pl.ds(group * 8, 8)] = rows

            @pl.loop(0, 8)
            def _(i):
                to = group * 8 + i

                @pl.when(to != here)
                def _():
                    send(
                        zs_r.at[half, to], zr_r.at[half, z * SLOTS + y], r_send, zr_sem.at[half],
                        (x, to),
                    )

        zr_r[half, pl.ds(z * SLOTS + y, 1)] = zs_r[half, pl.ds(here, 1)]

    def primary_in(k):
        @pl.when(c == 0)
        def _():
            rows_in(k)

    def put_owned():
        t0, t1 = iota((192, 192), 0), iota((192, 192), 1)
        place = ((t1 & 63) >> 2) * 12 + (t1 >> 6) * 4 + (t1 & 3)
        kept = (m_owns[0:1, 0:1] > 0.5) | (c == 1)
        table = onehot((t0 == place) & kept)
        for k in range(CHUNKS):
            for b in range(4):
                rows = jnp.concatenate(
                    [x_d[k, 256 * g + 64 * b : 256 * g + 64 * (b + 1)] for g in range(3)], axis=0
                )
                owned_ref[192 * b : 192 * (b + 1), k * WIDE : (k + 1) * WIDE] = dot(
                    table, rows
                ).astype(BF)

    def unpack(half):
        @pl.when(c == 0)
        def _():
            wait_recv(zr_r.at[half, pl.ds(0, 31)], zr_sem.at[half])

        @pl.when(c == 1)
        def _():
            wait_recv(zr_r.at[half, pl.ds(0, 32)], zr_sem.at[half])

        for q in range(4):
            rows = zr_r[half].reshape(512, 3 * NARROW)
            rows = dot(m_back[128 * q : 128 * (q + 1)], rows) * SCALE
            for g in range(3):
                for rr in range(4):
                    first = 512 * half + NARROW * q
                    update_ref[4 * g + rr, :, first : first + NARROW] = rows[
                        32 * rr : 32 * rr + MROW, NARROW * g : NARROW * (g + 1)
                    ]

    pack(0)
    pl.semaphore_wait(barrier, 16)
    for step in range(1, NZ):
        pl.semaphore_signal(all_in, 1, device_id=at(y, (z + step) % NZ, c), device_id_type=MESH)
    send_first(0)
    pack(1)
    send_first(1)
    send_combined(0)
    pack(2)
    send_first(2)
    pack_own(0)
    make_tables()
    load_momentum.wait()
    for k in range(PARTS):
        if k + 1 < PARTS:
            send_combined(k + 1)
        if k + 3 < PARTS:
            pack(k + 3)
            send_first(k + 3)
        if k + 1 < PARTS:
            pack_own(k + 1)
        gradient(k)
        if k == 0:
            pl.semaphore_wait(all_in, NZ - 1)
        rows_out(k)
        if k >= 2:
            primary_in(k - 2)
    rows_out_over(0)
    rows_out_over(1)
    primary_in(PARTS - 2)
    rows_out_over(2)
    rows_out_over(3)
    rows_out_over(4)
    rows_out_over(5)

    @pl.when(c == 0)
    def _():
        rows_in(PARTS - 1)
        finish(x_in, x_d, send_back, lambda: None)

    @pl.when(c == 1)
    def _():
        for k in range(PARTS):
            rows_in(k)
        finish(x_in, x_d, lambda k: None, lambda: None)

    put_owned()
    for half in range(2):
        unpack(half)

    wait_send(s_far, x_send.at[0])
    wait_send(s_direct, x_send.at[1])
    wait_send(s_comb, x_send.at[2])

    @pl.when(c == 0)
    def _():
        wait_send(zs_f.at[:, pl.ds(0, CHIPS - 1)], z_send.at[0])
        wait_send(zs_o, z_send.at[1])
        wait_send(zs_r.at[:, pl.ds(0, 63)], r_send)

    @pl.when(c == 1)
    def _():
        wait_send(zs_f, z_send.at[0])
        wait_send(zs_o.at[:, pl.ds(0, CHIPS - 1)], z_send.at[1])


def scratch():
    def vmem(*shape, dtype=BF):
        return pltpu.VMEM(shape, dtype)

    dma = pltpu.SemaphoreType.DMA
    x_half = (2, PARTS, 112, HALF)
    whole = (CHUNKS, F, WIDE)
    return [
        vmem(PARTS, 4, 112, 512, dtype=F32),
        vmem(12, MROW, D, dtype=F32),
        *[vmem(*x_half) for _ in range(6)],
        vmem(*x_half, dtype=F32),
        vmem(PARTS, 112, 512, dtype=F32),
        vmem(128, 512, dtype=F32),
        vmem(PARTS, CHIPS, 16, NARROW),
        vmem(PARTS, CHIPS, 16, NARROW),
        vmem(PARTS, 64, 16, NARROW),
        vmem(2, 64, 16, 3 * NARROW),
        vmem(2, CHIPS, 16, 3 * NARROW),
        vmem(*whole),
        vmem(*whole),
        vmem(*whole),
        vmem(F, F, dtype=F32),
        vmem(F, F),
        vmem(F, F),
        vmem(512, 512),
        vmem(512, 512),
        vmem(512, 512),
        vmem(8, 128, dtype=F32),
        dma((PARTS + 1,)),
        dma((3,)),
        dma((2, PARTS)),
        dma((2, PARTS)),
        dma((2, PARTS)),
        dma((2,)),
        dma(()),
        dma((2,)),
        dma((PARTS,)),
        pltpu.SemaphoreType.REGULAR,
    ]


def hand_over(*refs):
    srcs, dsts, sem = refs[:3], refs[3:6], refs[6]
    moves = []
    for i, (src, dst) in enumerate(zip(srcs, dsts)):
        rows = src.shape[0] // PIECES
        for piece in range(PIECES):
            part = pl.ds(piece * rows, rows)
            moves.append(pltpu.make_async_copy(src.at[part], dst.at[part], sem.at[i, piece]))
    for move in moves:
        move.start()
    for move in moves:
        move.wait()


def local(partial_grads, momentum, owners):
    grads = jnp.transpose(partial_grads[0], (1, 0, 2))
    held = jnp.transpose(momentum, (1, 0, 2))
    owners = owners.reshape(1, 112)
    vmem = pl.BlockSpec(memory_space=pltpu.VMEM)
    anywhere = pl.BlockSpec(memory_space=pl.ANY)
    outs = (
        jax.ShapeDtypeStruct((12, MROW, D), F32),
        jax.ShapeDtypeStruct((12, MROW, D), F32),
        jax.ShapeDtypeStruct((F, D), BF),
    )
    results = pl.pallas_call(
        kernel,
        out_shape=outs,
        in_specs=[anywhere, anywhere, vmem],
        out_specs=(vmem,) * 3,
        scratch_shapes=scratch(),
        compiler_params=pltpu.CompilerParams(
            collective_id=0, has_side_effects=True, vmem_limit_bytes=LIMIT << 20
        ),
    )(grads, held, owners)
    new_momentum, update, owned = pl.pallas_call(
        hand_over,
        out_shape=outs,
        in_specs=[vmem] * 3,
        out_specs=(anywhere,) * 3,
        scratch_shapes=[pltpu.SemaphoreType.DMA((3, PIECES))],
        compiler_params=pltpu.CompilerParams(vmem_limit_bytes=8 << 20),
    )(*results)
    return (
        jnp.transpose(new_momentum, (1, 0, 2)),
        jnp.transpose(update, (1, 0, 2)),
        owned[None, None],
    )


def solution(mesh):
    return jax.shard_map(
        local,
        mesh=mesh,
        in_specs=(P("dp", None, "shard", None), P("dp", "shard", None), P()),
        out_specs=(P("dp", "shard", None), P("dp", "shard", None), P("dp", "shard", None, None)),
        check_vma=False,
    )
```

```python
import functools
import math

import jax
import jax.numpy as jnp
from jax import lax
from jax.experimental import pallas as pl
from jax.experimental.pallas import tpu as pltpu
from jax.sharding import PartitionSpec as P


MESH = pl.DeviceIdType.MESH
BF = jnp.bfloat16
F32 = jnp.float32
I32 = jnp.int32

D, F = 1024, 768
NX, NY, NZ = 4, 4, 8
MROW = 28
CHUNKS, WIDE = 4, 256
PARTS, HALF, NARROW = 6, 256, 128
CHIPS = 32
SLOTS = 4
PIECES = 4
LIMIT = 48
SCALE = 0.2 * math.sqrt(max(F, D))

momentum_decay = 0.95
epsilon_norm = 1e-07
coeff_first = 3.4445
coeff_second = -4.775
coeff_third = 2.0315


def iota(shape, axis):
    return lax.broadcasted_iota(I32, shape, axis)


def onehot(cond):
    return jnp.where(cond, 1.0, 0.0).astype(BF)


def dot(a, b):
    return jnp.dot(a, b, preferred_element_type=F32)


def dot_t(a, b):
    return lax.dot_general(a, b, (((1,), (1,)), ((), ())), preferred_element_type=F32)


def routes(owner, chip_here):
    r0, r1 = iota((128, 128), 0), iota((128, 128), 1)
    owner = jnp.broadcast_to(owner[0:1], (128, 128))
    valid = r1 < MROW
    chip = jnp.where(valid, ((owner >> 1) & 7) * SLOTS + (owner >> 4), -1).astype(F32)
    core = jnp.where(valid, owner & 1, -1)
    first, second = core == 0, core == 1
    diag, before = r0 == r1, r0 < r1
    r0f = r0.astype(F32)

    def over_rows(cond, value=1.0):
        return jnp.sum(jnp.where(cond, value, 0.0), axis=0, keepdims=True)

    def over_lanes(cond, value=1.0):
        return jnp.sum(jnp.where(cond, value, 0.0), axis=1, keepdims=True)

    second_col = over_lanes(diag & second)
    nth = over_rows(before & (second_col > 0.5))
    taken = over_lanes(first & (chip == r0f))
    free = jnp.where((r0[:, 0:1] < NZ * SLOTS) & (taken < 0.5), 1.0, 0.0)
    free_row = over_rows(diag & (free > 0.5))
    free_before = over_lanes((r1 < r0) & (free_row > 0.5))
    away = over_rows((free > 0.5) & (free_before == nth), r0f)
    first, second, valid, chip = first[0:1], second[0:1], valid[0:1], chip[0:1]
    code = jnp.where(first, chip, jnp.where(second, away, -1.0))
    code_over = jnp.where(second, chip, -1.0)
    owns = jnp.sum(
        jnp.where(first & (chip == chip_here.astype(F32)), 1.0, 0.0), axis=1, keepdims=True
    )

    def tiled(row):
        row = jnp.where(valid, row, -1.0)
        wide = jnp.broadcast_to(row, (8, 128))
        out = wide
        for turn in (1, 2, 3):
            lane = iota((8, 128), 1)
            out = jnp.where((lane >> 5) == turn, pltpu.roll(wide, 32 * turn, 1), out)
        return out[0:1]

    f0, f1 = iota((512, 128), 0), iota((512, 128), 1)
    same_row = ((f0 >> 2) & 3) == (f1 >> 5)
    chip_at = (f0 >> 4).astype(F32)

    def outward(row):
        meant = same_row & (tiled(row) == chip_at)
        return [onehot(meant & ((f0 & 3) == q)) for q in range(4)]

    forward, forward_over = outward(code), outward(code_over)
    code_col = jnp.sum(
        jnp.where(r1 == (r0 & 31), jnp.broadcast_to(code, (128, 128)), 0.0), axis=1, keepdims=True
    )
    code_col = jnp.where((r0[:, 0:1] & 31) < MROW, code_col, -1.0)
    b0, b1 = iota((128, 512), 0), iota((128, 512), 1)
    whose = ((b0 >> 5) == ((b1 >> 2) & 3)) & (code_col == (b1 >> 4).astype(F32))
    back = [onehot(whose & ((b1 & 3) == q)) for q in range(4)]
    return forward, forward_over, back, owns


def kernel(
    grads_hbm,
    momentum_hbm,
    owners_ref,
    newm_ref,
    update_ref,
    owned_ref,
    grads,
    momentum,
    s_direct,
    s_far,
    s_comb,
    r_direct,
    r_far,
    r_comb,
    part,
    own,
    nest,
    zs_f,
    zs_o,
    raw,
    zs_r,
    zr_r,
    x_in,
    x_d,
    x_b,
    gram_f,
    gram_b,
    poly_b,
    m_forward,
    m_over,
    m_back,
    m_owns,
    load_sem,
    x_send,
    direct_sem,
    far_sem,
    comb_sem,
    z_send,
    r_send,
    zr_sem,
    in_sem,
    all_in,
):
    x = lax.axis_index("dp")
    here = lax.axis_index("shard")
    y, z, c = here // 16, (here // 2) % NZ, here % 2
    e = 2 * y + c
    right, left, far = (x + 1) % NX, (x + 3) % NX, (x + 2) % NX

    def at(y_, z_, c_):
        return (x, (y_ * NZ + z_) * 2 + c_)

    def send(src, dst, send_sem, recv_sem, device):
        pltpu.make_async_remote_copy(
            src_ref=src, dst_ref=dst, send_sem=send_sem, recv_sem=recv_sem,
            device_id=device, device_id_type=MESH,
        ).start()

    def wait_recv(ref, sem):
        pltpu.make_async_remote_copy(
            src_ref=ref, dst_ref=ref, send_sem=sem, recv_sem=sem,
            device_id=(x, here), device_id_type=MESH,
        ).wait_recv()

    def wait_send(ref, sem):
        pltpu.make_async_remote_copy(
            src_ref=ref, dst_ref=ref, send_sem=sem, recv_sem=sem,
            device_id=(x, here), device_id_type=MESH,
        ).wait_send()

    def load(k):
        return pltpu.make_async_copy(
            grads_hbm.at[pl.ds(4 * (k % 3), 4), :, pl.ds(512 * (k // 3), 512)],
            grads.at[k],
            load_sem.at[k],
        )

    load_momentum = pltpu.make_async_copy(momentum_hbm, momentum, load_sem.at[PARTS])
    for k in range(PARTS):
        load(k).start()
    load_momentum.start()

    barrier = pltpu.get_barrier_semaphore()
    for device in ((right, here), (left, here)):
        pl.semaphore_signal(barrier, 1, device_id=device, device_id_type=MESH)
    for step in range(1, NZ):
        pl.semaphore_signal(barrier, 1, device_id=at(y, (z + step) % NZ, c), device_id_type=MESH)
    for step in range(1, 8):
        other = (e + step) % 8
        pl.semaphore_signal(
            barrier, 1, device_id=at(other // 2, z, other % 2), device_id_type=MESH
        )

    def make_tables():
        owner = jnp.concatenate([owners_ref[...], jnp.zeros((1, 16), I32)], axis=1)
        owner = pltpu.roll(jnp.broadcast_to(owner, (8, 128)), (128 - MROW * x) % 128, 1)
        forward, forward_over, back, owns = routes(owner, z * SLOTS + y)
        for q in range(4):
            m_forward[:, 128 * q : 128 * (q + 1)] = forward[q]
            m_over[:, 128 * q : 128 * (q + 1)] = forward_over[q]
            m_back[128 * q : 128 * (q + 1)] = back[q]
        m_owns[...] = jnp.broadcast_to(owns, (8, 128))
        nest[...] = jnp.zeros_like(nest)

    p0, p1 = iota((112, 128), 0), iota((112, 128), 1)
    quarter = (
        jnp.where(p0 >= 28, 1, 0) + jnp.where(p0 >= 56, 1, 0) + jnp.where(p0 >= 84, 1, 0)
    )

    def packing(parity):
        return onehot(p1 == p0 + 4 * quarter + 4 * parity)

    def window(k, to, table):
        start = pl.multiple_of(((MROW * to) // 8) * 8, 8)
        rows = grads[k, :, pl.ds(start, 32), :].astype(BF).reshape(128, 2 * HALF)
        return dot(table, rows)

    def pack(k):
        load(k).wait()
        odd = packing((x + 1) % 2)
        even = packing(x % 2)
        v = window(k, far, even).astype(BF)
        s_far[0, k] = v[:, :HALF]
        s_far[1, k] = v[:, HALF:]
        v = window(k, right, odd)
        part[0, k] = v[:, :HALF]
        s_direct[0, k] = v[:, HALF:].astype(BF)
        v = window(k, left, odd)
        part[1, k] = v[:, HALF:]
        s_direct[1, k] = v[:, :HALF].astype(BF)

    def pack_own(k):
        own[k] = window(k, x, packing(x % 2))

    towards = ((right, here), (left, here))

    def send_first(k):
        for way in range(2):
            send(s_far.at[way, k], r_far.at[way, k], x_send.at[0], far_sem.at[way, k], towards[way])
        for way in range(2):
            send(
                s_direct.at[way, k], r_direct.at[way, k], x_send.at[1], direct_sem.at[way, k],
                towards[way],
            )

    def send_combined(k):
        for way in range(2):
            wait_recv(r_far.at[way, k], far_sem.at[way, k])
            s_comb[way, k] = (part[way, k] + r_far[way, k].astype(F32)).astype(BF)
            send(
                s_comb.at[way, k], r_comb.at[way, k], x_send.at[2], comb_sem.at[way, k],
                towards[way],
            )

    def gradient(k):
        for way in range(2):
            wait_recv(r_direct.at[way, k], direct_sem.at[way, k])
            wait_recv(r_comb.at[way, k], comb_sem.at[way, k])
        low = own[k, :, :HALF] + r_direct[1, k].astype(F32) + r_comb[0, k].astype(F32)
        high = own[k, :, HALF:] + r_direct[0, k].astype(F32) + r_comb[1, k].astype(F32)
        own[k, :, :HALF] = low
        own[k, :, HALF:] = high
        g, half = k % 3, k // 3
        cols = slice(512 * half, 512 * (half + 1))
        for rr in range(4):
            total = own[k, MROW * rr : MROW * (rr + 1), :]
            moved = momentum_decay * momentum[4 * g + rr, :, cols] + total
            newm_ref[4 * g + rr, :, cols] = moved
            nest[32 * rr : 32 * rr + MROW, :] = total + momentum_decay * moved

    def send_out(k, zs, core, sem):
        @pl.loop(0, CHIPS)
        def _(i):
            j = i // 4
            to_z = (z + 4 + (1 - 2 * (j % 2)) * ((j + 1) // 2)) % NZ
            to_y = (y + i) % NY

            @pl.when(jnp.logical_or(i != 28, c != core))
            def _():
                send(
                    zs.at[k, to_z * SLOTS + to_y], raw.at[k, here], sem, in_sem.at[k],
                    at(to_y, to_z, core),
                )

        @pl.when(c == core)
        def _():
            raw[k, pl.ds(here, 1)] = zs[k, pl.ds(z * SLOTS + y, 1)]

    def rows_out(k):
        rows = nest[...].astype(BF)
        rows = jnp.concatenate([rows[:, NARROW * q : NARROW * (q + 1)] for q in range(4)], axis=0)
        zs_f[k] = dot(m_forward[...], rows).astype(BF).reshape(CHIPS, 16, NARROW)
        send_out(k, zs_f, 0, z_send.at[0])
        zs_o[k] = dot(m_over[...], rows).astype(BF).reshape(CHIPS, 16, NARROW)

    def rows_out_over(k):
        send_out(k, zs_o, 1, z_send.at[1])

    i0, i1 = iota((128, 128), 0), iota((128, 128), 1)
    to_columns = lambda: onehot(i1 == ((i0 & 31) << 2) + (i0 >> 5))
    from_columns = lambda: onehot(i0 == ((i1 & 31) << 2) + (i1 >> 5))

    def rows_in(k):
        wait_recv(raw.at[k, pl.ds(0, 63)], in_sem.at[k])
        g, half = k % 3, k // 3
        rows = jnp.concatenate(
            [raw[k, 8 * i : 8 * (i + 1)].reshape(128, NARROW) for i in range(8)], axis=1
        )
        rows = dot(to_columns(), rows).astype(BF)
        for q in range(4):
            for i in range(8):
                first = 256 * g + 32 * i
                x_in[
                    2 * half + q // 2, first : first + 32,
                    NARROW * (q % 2) : NARROW * (q % 2 + 1),
                ] = rows[32 * q : 32 * (q + 1), NARROW * i : NARROW * (i + 1)]
        if g == 2:
            add_gram(x_in, half)

    def matrix(ref, k):
        return ref[k]

    blocks = [(i, j) for i in range(3) for j in range(i, 3)]

    def block(ref, i, j):
        return ref.at[256 * i : 256 * (i + 1), 256 * j : 256 * (j + 1)]

    def add_gram(src, half):
        for i, j in blocks:
            new = 0.0
            for k in (2 * half, 2 * half + 1):
                rows = matrix(src, k)
                new = new + dot_t(rows[256 * i : 256 * (i + 1)], rows[256 * j : 256 * (j + 1)])
            into = block(gram_f, i, j)
            into[...] = new if half == 0 else into[...] + new

    def put_gram(i, j, value):
        value = value.astype(BF)
        block(gram_b, i, j)[...] = value
        if i != j:
            block(gram_b, j, i)[...] = value.T

    def whole_gram(src):
        for i, j in blocks:
            total = 0.0
            for k in range(CHUNKS):
                rows = matrix(src, k)
                total = total + dot_t(
                    rows[256 * i : 256 * (i + 1)], rows[256 * j : 256 * (j + 1)]
                )
            put_gram(i, j, total)

    def poly():
        for i, j in blocks:
            square = dot(
                gram_b[256 * i : 256 * (i + 1), :], gram_b[:, 256 * j : 256 * (j + 1)]
            )
            value = coeff_second * block(gram_b, i, j)[...].astype(F32) + coeff_third * square
            value = value.astype(BF)
            block(poly_b, i, j)[...] = value
            if i != j:
                block(poly_b, j, i)[...] = value.T

    def advance(src, dst, k, scale=None):
        rows = matrix(src, k)
        out = coeff_first * rows.astype(F32) + dot(poly_b[...], rows)
        if scale is not None:
            out = out * scale
        dst[k] = out.astype(BF)

    def finish(src, dst, done, between):
        d0, d1 = iota((256, 256), 0), iota((256, 256), 1)
        squares = 0.0
        for i in range(3):
            squares = squares + jnp.sum(jnp.where(d0 == d1, block(gram_f, i, i)[...], 0.0))
        inverse = 1.0 / (jnp.sqrt(squares) + epsilon_norm)
        for i, j in blocks:
            put_gram(i, j, block(gram_f, i, j)[...] * (inverse * inverse))
        poly()
        for k in range(CHUNKS):
            advance(src, x_b, k, inverse)
        between()
        whole_gram(x_b)
        poly()
        for k in range(CHUNKS):
            advance(x_b, dst, k)
            done(k)

    def send_back(k):
        if k % 2 == 0:
            return
        half = k // 2
        table = from_columns()

        @pl.loop(0, 8)
        def _(step):
            group = (here // 8 + step) % 8
            rows = jnp.concatenate(
                [
                    jnp.concatenate(
                        [
                            x_d[
                                k - 1 + q // 2,
                                pl.ds(pl.multiple_of(256 * g + 32 * group, 32), 32),
                                NARROW * (q % 2) : NARROW * (q % 2 + 1),
                            ]
                            for g in range(3)
                        ],
                        axis=1,
                    )
                    for q in range(4)
                ],
                axis=0,
            )
            rows = dot(table, rows).astype(BF).reshape(8, 16, 3 * NARROW)
            zs_r[half, pl.ds(group * 8, 8)] = rows

            @pl.loop(0, 8)
            def _(i):
                to = group * 8 + i

                @pl.when(to != here)
                def _():
                    send(
                        zs_r.at[half, to], zr_r.at[half, z * SLOTS + y], r_send, zr_sem.at[half],
                        (x, to),
                    )

        zr_r[half, pl.ds(z * SLOTS + y, 1)] = zs_r[half, pl.ds(here, 1)]

    def primary_in(k):
        @pl.when(c == 0)
        def _():
            rows_in(k)

    def put_owned():
        t0, t1 = iota((192, 192), 0), iota((192, 192), 1)
        place = ((t1 & 63) >> 2) * 12 + (t1 >> 6) * 4 + (t1 & 3)
        kept = (m_owns[0:1, 0:1] > 0.5) | (c == 1)
        table = onehot((t0 == place) & kept)
        for k in range(CHUNKS):
            for b in range(4):
                rows = jnp.concatenate(
                    [x_d[k, 256 * g + 64 * b : 256 * g + 64 * (b + 1)] for g in range(3)], axis=0
                )
                owned_ref[192 * b : 192 * (b + 1), k * WIDE : (k + 1) * WIDE] = dot(
                    table, rows
                ).astype(BF)

    def unpack(half):
        @pl.when(c == 0)
        def _():
            wait_recv(zr_r.at[half, pl.ds(0, 31)], zr_sem.at[half])

        @pl.when(c == 1)
        def _():
            wait_recv(zr_r.at[half, pl.ds(0, 32)], zr_sem.at[half])

        for q in range(4):
            rows = zr_r[half].reshape(512, 3 * NARROW)
            rows = dot(m_back[128 * q : 128 * (q + 1)], rows) * SCALE
            for g in range(3):
                for rr in range(4):
                    first = 512 * half + NARROW * q
                    update_ref[4 * g + rr, :, first : first + NARROW] = rows[
                        32 * rr : 32 * rr + MROW, NARROW * g : NARROW * (g + 1)
                    ]

    pack(0)
    pl.semaphore_wait(barrier, 16)
    for step in range(1, NZ):
        pl.semaphore_signal(all_in, 1, device_id=at(y, (z + step) % NZ, c), device_id_type=MESH)
    send_first(0)
    pack(1)
    send_first(1)
    send_combined(0)
    pack(2)
    send_first(2)
    pack_own(0)
    make_tables()
    load_momentum.wait()
    for k in range(PARTS):
        if k + 1 < PARTS:
            send_combined(k + 1)
        if k + 3 < PARTS:
            pack(k + 3)
            send_first(k + 3)
        if k + 1 < PARTS:
            pack_own(k + 1)
        gradient(k)
        if k == 0:
            pl.semaphore_wait(all_in, NZ - 1)
        rows_out(k)
        if k == 0 or k == 2:
            rows_out_over(k // 2)
        if k >= 2:
            primary_in(k - 2)
    rows_out_over(2)
    primary_in(PARTS - 2)
    rows_out_over(3)
    rows_out_over(4)
    rows_out_over(5)

    @pl.when(c == 0)
    def _():
        rows_in(PARTS - 1)
        finish(x_in, x_d, send_back, lambda: None)

    @pl.when(c == 1)
    def _():
        for k in range(PARTS):
            rows_in(k)
        finish(x_in, x_d, lambda k: None, lambda: None)

    put_owned()
    for half in range(2):
        unpack(half)

    wait_send(s_far, x_send.at[0])
    wait_send(s_direct, x_send.at[1])
    wait_send(s_comb, x_send.at[2])

    @pl.when(c == 0)
    def _():
        wait_send(zs_f.at[:, pl.ds(0, CHIPS - 1)], z_send.at[0])
        wait_send(zs_o, z_send.at[1])
        wait_send(zs_r.at[:, pl.ds(0, 63)], r_send)

    @pl.when(c == 1)
    def _():
        wait_send(zs_f, z_send.at[0])
        wait_send(zs_o.at[:, pl.ds(0, CHIPS - 1)], z_send.at[1])


def scratch():
    def vmem(*shape, dtype=BF):
        return pltpu.VMEM(shape, dtype)

    dma = pltpu.SemaphoreType.DMA
    x_half = (2, PARTS, 112, HALF)
    whole = (CHUNKS, F, WIDE)
    return [
        vmem(PARTS, 4, 112, 512, dtype=F32),
        vmem(12, MROW, D, dtype=F32),
        *[vmem(*x_half) for _ in range(6)],
        vmem(*x_half, dtype=F32),
        vmem(PARTS, 112, 512, dtype=F32),
        vmem(128, 512, dtype=F32),
        vmem(PARTS, CHIPS, 16, NARROW),
        vmem(PARTS, CHIPS, 16, NARROW),
        vmem(PARTS, 64, 16, NARROW),
        vmem(2, 64, 16, 3 * NARROW),
        vmem(2, CHIPS, 16, 3 * NARROW),
        vmem(*whole),
        vmem(*whole),
        vmem(*whole),
        vmem(F, F, dtype=F32),
        vmem(F, F),
        vmem(F, F),
        vmem(512, 512),
        vmem(512, 512),
        vmem(512, 512),
        vmem(8, 128, dtype=F32),
        dma((PARTS + 1,)),
        dma((3,)),
        dma((2, PARTS)),
        dma((2, PARTS)),
        dma((2, PARTS)),
        dma((2,)),
        dma(()),
        dma((2,)),
        dma((PARTS,)),
        pltpu.SemaphoreType.REGULAR,
    ]


def hand_over(*refs):
    srcs, dsts, sem = refs[:3], refs[3:6], refs[6]
    moves = []
    for i, (src, dst) in enumerate(zip(srcs, dsts)):
        rows = src.shape[0] // PIECES
        for piece in range(PIECES):
            part = pl.ds(piece * rows, rows)
            moves.append(pltpu.make_async_copy(src.at[part], dst.at[part], sem.at[i, piece]))
    for move in moves:
        move.start()
    for move in moves:
        move.wait()


def local(partial_grads, momentum, owners):
    grads = jnp.transpose(partial_grads[0], (1, 0, 2))
    held = jnp.transpose(momentum, (1, 0, 2))
    owners = owners.reshape(1, 112)
    vmem = pl.BlockSpec(memory_space=pltpu.VMEM)
    anywhere = pl.BlockSpec(memory_space=pl.ANY)
    outs = (
        jax.ShapeDtypeStruct((12, MROW, D), F32),
        jax.ShapeDtypeStruct((12, MROW, D), F32),
        jax.ShapeDtypeStruct((F, D), BF),
    )
    results = pl.pallas_call(
        kernel,
        out_shape=outs,
        in_specs=[anywhere, anywhere, vmem],
        out_specs=(vmem,) * 3,
        scratch_shapes=scratch(),
        compiler_params=pltpu.CompilerParams(
            collective_id=0, has_side_effects=True, vmem_limit_bytes=LIMIT << 20
        ),
    )(grads, held, owners)
    new_momentum, update, owned = pl.pallas_call(
        hand_over,
        out_shape=outs,
        in_specs=[vmem] * 3,
        out_specs=(anywhere,) * 3,
        scratch_shapes=[pltpu.SemaphoreType.DMA((3, PIECES))],
        compiler_params=pltpu.CompilerParams(vmem_limit_bytes=8 << 20),
    )(*results)
    return (
        jnp.transpose(new_momentum, (1, 0, 2)),
        jnp.transpose(update, (1, 0, 2)),
        owned[None, None],
    )


def solution(mesh):
    return jax.shard_map(
        local,
        mesh=mesh,
        in_specs=(P("dp", None, "shard", None), P("dp", "shard", None), P()),
        out_specs=(P("dp", "shard", None), P("dp", "shard", None), P("dp", "shard", None, None)),
        check_vma=False,
    )
```
